32 devices in a mesh: clip: 8 (over z, x), seq: 4 (over y, core).
Axes of the slice: x: 2, y: 2, z: 4, core: 2. Of those that a mesh axis runs over, the one named last changes fastest.
Arguments:
- tokens: bfloat16 [8, 2048, 768], P('clip', 'seq'), may hold values from -6 to 6
- out_grad: bfloat16 [8, 2048, 768], P('clip', 'seq'), may hold values from -6144 to 6144
- saved_logits: bfloat16 [8, 2048, 128], P('clip', 'seq'), may hold values from -14 to 400
- slot_params: bfloat16 [768, 128], P(None, 'seq'), may hold values from -0.21875 to 0.21875
- slot_inputs: bfloat16 [8, 128, 768], P(None, ('clip', 'seq')), may hold values from -6 to 6
- slot_outputs: bfloat16 [8, 128, 768], P('clip', 'seq'), may hold values from -0.119628906 to 0.119628906
- expert_in: bfloat16 [32, 768, 3072], P(('clip', 'seq')), may hold values from -0.21875 to 0.21875
- expert_out: bfloat16 [32, 3072, 768], P(('clip', 'seq')), may hold values from -0.109375 to 0.109375
Outputs:
- token_grad: bfloat16 [8, 2048, 768], P('clip', 'seq')
The draws below stay inside these ranges and needn't reach their ends.
All inputs are finite; a program needn't handle non-finite values.
Results may differ from the reference program's by a relative error of at most 0.023.
Values may be sent and summed in bfloat16 or wider, within the bound.
No kernel may reach another device: no remote copies, remote signals or barrier semaphores. Data moves between devices by JAX's collectives and lax.ppermute only.
A program may use at most 64 MiB of HBM per device.

```python
import math
import jax
import jax.numpy as jnp
from jax import lax

D = 768
HID = 3072
SLOTS = 4
EXPERTS = 32
CLIPS = 8
LENGTH = 2048
SLOTS_CLIP = 128


def draw_saved_logits(key, part):
    keys = jax.random.split(jax.random.fold_in(key, 7), 3)
    position = jnp.arange(LENGTH, dtype=jnp.float32) / LENGTH
    shape = (CLIPS, LENGTH, SLOTS_CLIP)
    noise_draw = jnp.clip(jax.random.normal(keys[0], shape, jnp.float32), -4.0, 4.0)
    row_scale = jnp.exp(jax.random.uniform(keys[1], (CLIPS, LENGTH, 1), jnp.float32, math.log(0.5), math.log(2.0)))
    col_scale = jnp.exp(jax.random.uniform(keys[2], (CLIPS, 1, SLOTS_CLIP), jnp.float32, math.log(0.95), math.log(1.05)))
    ramp_term = math.log(3.0) * position
    return (noise_draw * row_scale * col_scale + ramp_term[None, :, None]).astype(jnp.bfloat16)


def block_levels(key, dims, cuts, smallest, top_value):
    loudness, own = 1.0, jax.random.fold_in(key, 6)
    for dim, shards_of in cuts:
        draws = jnp.exp(jax.random.uniform(jax.random.fold_in(own, dim), (shards_of,), jnp.float32, smallest / len(cuts), top_value / len(cuts)))
        loudness = loudness * jnp.repeat(draws, dims[dim] // shards_of).reshape([-1 if axis == dim else 1 for axis in range(len(dims))])
    return loudness


def gaussian(key, extent, scale, most, cuts=(), kind=jnp.bfloat16):
    level = block_levels(key, extent, cuts, -0.22, 0.18) if cuts else 1.0
    drawn = jax.random.normal(key, extent, jnp.float32) * scale * level
    return jnp.minimum(jnp.maximum(drawn, -most), most).astype(kind)


def setup_inputs(seed: int = 0) -> dict:
    key_list = jax.random.split(jax.random.key(seed), 9)
    return {
        "tokens": gaussian(key_list[0], (CLIPS, LENGTH, D), 1.0, 6.0, ((0, 8), (1, 4))),
        "out_grad": gaussian(key_list[1], (CLIPS, LENGTH, D), 1024.0, 6144.0, ((0, 8), (1, 4))),
        "saved_logits": draw_saved_logits(jax.random.fold_in(key_list[8], 71), 0),
        "slot_params": gaussian(key_list[3], (D, SLOTS_CLIP), D ** -0.5, 0.21875, ((1, 4),)),
        "slot_inputs": gaussian(key_list[4], (CLIPS, SLOTS_CLIP, D), 1.0, 6.0, ((1, 32),)),
        "slot_outputs": gaussian(key_list[5], (CLIPS, SLOTS_CLIP, D), 0.02, 0.119628906, ((0, 8), (1, 4))),
        "expert_in": gaussian(key_list[6], (EXPERTS, D, HID), D ** -0.5, 0.21875, ((0, 32),)),
        "expert_out": gaussian(key_list[7], (EXPERTS, HID, D), HID ** -0.5, 0.109375, ((0, 32),)),
    }


def softmax_pair(logit_raw):
    scores = logit_raw.astype(jnp.float32)
    combine = jax.nn.softmax(scores, axis=1)
    dispatch = jax.nn.softmax(scores, axis=0)
    return (combine, dispatch)

def combine_part(combine, out_cot, slot_out):
    comb_cot = jnp.dot(out_cot, slot_out.T, preferred_element_type=jnp.float32)
    return combine * (comb_cot - lax.optimization_barrier(jnp.sum(combine * comb_cot, axis=1, keepdims=True)))

def front_pass(operands):
    logit_raw, out_cot = operands
    combine, dispatch = softmax_pair(logit_raw)
    return jnp.dot(combine.astype(jnp.bfloat16).T, out_cot, preferred_element_type=jnp.float32).astype(jnp.bfloat16)

def expert_grad(operands):
    slot_in, slot_cot, weight_in, weight_out = operands
    hidden = jnp.dot(slot_in, weight_in, preferred_element_type=jnp.float32)
    act_cot = jnp.dot(slot_cot, weight_out.T, preferred_element_type=jnp.float32)
    unused, pull_back = jax.vjp(jax.nn.gelu, hidden)
    hidden_cot = pull_back(act_cot)[0].astype(jnp.bfloat16)
    return jnp.dot(hidden_cot, weight_in.T, preferred_element_type=jnp.float32).astype(jnp.bfloat16)

def reference(tokens, out_grad, saved_logits, slot_params, slot_inputs, slot_outputs, expert_in, expert_out):
    slot_cot = lax.map(front_pass, (saved_logits, out_grad))
    stacked_in = slot_inputs.reshape(CLIPS, EXPERTS, SLOTS, D).transpose(1, 0, 2, 3).reshape(EXPERTS, CLIPS * SLOTS, D)
    stacked_cot = slot_cot.reshape(CLIPS, EXPERTS, SLOTS, D).transpose(1, 0, 2, 3).reshape(EXPERTS, CLIPS * SLOTS, D)
    stacked_grad = lax.map(expert_grad, (stacked_in, stacked_cot, expert_in, expert_out))
    slot_grad = stacked_grad.reshape(EXPERTS, CLIPS, SLOTS, D).transpose(1, 0, 2, 3).reshape(CLIPS, EXPERTS * SLOTS, D)

    def back_pass(operands):
        tok_feats, out_cot, logit_raw, slot_out, grads = operands
        combine, dispatch = softmax_pair(logit_raw)
        comb_logit = combine_part(combine, out_cot, slot_out)
        disp_cot = jnp.dot(tok_feats, grads.T, preferred_element_type=jnp.float32)
        col_sums = lax.optimization_barrier(jnp.sum(dispatch * disp_cot, axis=0, keepdims=True))
        disp_logit = dispatch * (disp_cot - col_sums)
        logit_grad = (comb_logit + disp_logit).astype(jnp.bfloat16)
        direct = jnp.dot(dispatch.astype(jnp.bfloat16), grads, preferred_element_type=jnp.float32)
        through = jnp.dot(logit_grad, slot_params.T, preferred_element_type=jnp.float32)
        return (direct + through).astype(jnp.bfloat16)
    return lax.map(back_pass, (tokens, out_grad, saved_logits, slot_outputs, slot_grad))
```

```python
import jax
import jax.numpy as jnp
from jax import lax
from jax.sharding import PartitionSpec as P

BOTH = ("clip", "seq")


def on_device(
    tokens, out_grad, saved_logits, slot_params, slot_inputs, slot_outputs, expert_in, expert_out
):
    clip_count = lax.axis_size("clip")
    seq_count = lax.axis_size("seq")
    tok_feats = tokens[0]
    out_cot = out_grad[0]
    scores = saved_logits[0].astype(jnp.float32)
    width = tok_feats.shape[1]
    slot_total = scores.shape[1]
    clip_total = slot_inputs.shape[0]
    local_slots = slot_inputs.shape[1]
    expert_block = expert_in.shape[0]
    slot_each = local_slots // expert_block
    combine = jax.nn.softmax(scores, axis=1)
    partial_cot = jnp.einsum(
        "ts,td->sd", combine.astype(jnp.bfloat16), out_cot, preferred_element_type=jnp.float32
    )
    blocks = partial_cot.astype(jnp.bfloat16).reshape(
        clip_count * seq_count, local_slots, width
    )
    received = lax.all_to_all(blocks, BOTH, split_axis=0, concat_axis=0, tiled=True)
    seq_slots = slot_params.shape[1]
    packed = jnp.concatenate([slot_params.T, slot_outputs[0]], axis=0)
    packed_all = lax.all_gather(packed, "seq", axis=0)
    param_all = packed_all[:, :seq_slots].reshape(slot_total, width)
    slot_out = packed_all[:, seq_slots:].reshape(slot_total, width)
    local_max = jnp.max(scores, axis=0)
    local_sum = jnp.sum(jnp.exp(scores - local_max), axis=0)
    stats = lax.all_gather(jnp.stack([local_max, local_sum]), "seq")
    col_max = jnp.max(stats[:, 0], axis=0)
    col_sum = jnp.sum(stats[:, 1] * jnp.exp(stats[:, 0] - col_max), axis=0)
    dispatch = jnp.exp(scores - col_max) / col_sum
    comb_cot = jnp.einsum("td,sd->ts", out_cot, slot_out, preferred_element_type=jnp.float32)
    comb_logit = combine * (comb_cot - jnp.sum(combine * comb_cot, axis=1, keepdims=True))
    expert_feed = slot_inputs.reshape(clip_total, expert_block, slot_each, width)
    hidden = jnp.einsum(
        "cejd,edh->cejh", expert_feed, expert_in, preferred_element_type=jnp.float32
    )
    expert_cot = received.reshape(clip_count, seq_count, expert_block, slot_each, width)
    expert_cot = jnp.sum(expert_cot.astype(jnp.float32), axis=1).astype(jnp.bfloat16)
    act_cot = jnp.einsum(
        "cejd,ehd->cejh", expert_cot, expert_out, preferred_element_type=jnp.float32
    )
    unused, pull_back = jax.vjp(jax.nn.gelu, hidden)
    hidden_cot = pull_back(act_cot)[0].astype(jnp.bfloat16)
    local_grad = jnp.einsum(
        "cejh,edh->cejd", hidden_cot, expert_in, preferred_element_type=jnp.float32
    ).astype(jnp.bfloat16)
    local_grad = local_grad.reshape(clip_count, 1, local_slots, width)
    copies = jnp.broadcast_to(local_grad, (clip_count, seq_count, local_slots, width))
    slot_grad = lax.all_to_all(
        copies.reshape(clip_count * seq_count, local_slots, width),
        BOTH,
        split_axis=0,
        concat_axis=0,
        tiled=True,
    ).reshape(slot_total, width)
    dispatch_b = dispatch.astype(jnp.bfloat16)
    direct = jnp.dot(dispatch_b, slot_grad, preferred_element_type=jnp.float32)
    disp_cot = jnp.einsum("td,sd->ts", tok_feats, slot_grad, preferred_element_type=jnp.float32)
    slot_dots = lax.psum(jnp.sum(dispatch * disp_cot, axis=0), "seq")
    disp_logit = dispatch * (disp_cot - slot_dots)
    logit_grad = (comb_logit + disp_logit).astype(jnp.bfloat16)
    through = jnp.einsum("ts,sd->td", logit_grad, param_all, preferred_element_type=jnp.float32)
    return (direct + through).astype(jnp.bfloat16)[None]


def solution(mesh):
    placed = (
        P("clip", "seq", None),
        P("clip", "seq", None),
        P("clip", "seq", None),
        P(None, "seq"),
        P(None, BOTH, None),
        P("clip", "seq", None),
        P(BOTH, None, None),
        P(BOTH, None, None),
    )
    return jax.shard_map(
        on_device, mesh=mesh, in_specs=placed, out_specs=P("clip", "seq", None), check_vma=False
    )
```

```python
import jax
import jax.numpy as jnp
from jax import lax
from jax.sharding import PartitionSpec as P

BOTH = ("clip", "seq")


def swap(value, bit):
    count = lax.axis_size("seq")
    return lax.ppermute(value, "seq", [(i, i ^ bit) for i in range(count)])


def pack_stats(highest, total, width):
    part0 = lax.reduce_precision(total, 8, 7)
    part1 = lax.reduce_precision(total - part0, 8, 7)
    part2 = total - part0 - part1
    flat = jnp.concatenate([highest, part0, part1, part2]).astype(jnp.bfloat16)
    rows = -(-flat.size // (8 * width)) * 8
    return jnp.pad(flat, (0, rows * width - flat.size)).reshape(rows, width)


def unpack_stats(rows, slot_total):
    parts = rows.reshape(-1)[: 4 * slot_total].astype(jnp.float32).reshape(4, slot_total)
    return parts[0], parts[1] + parts[2] + parts[3]


def merge(mine, theirs):
    highest = jnp.maximum(mine[0], theirs[0])
    scale_a, scale_b = jnp.exp(mine[0] - highest), jnp.exp(theirs[0] - highest)
    return highest, mine[1] * scale_a + theirs[1] * scale_b, scale_a, scale_b


def seq_exchange(highest, total, sums, static_rows):
    width = sums.shape[1]
    slot_total = sums.shape[0]
    count = lax.axis_size("seq")
    me = lax.axis_index("seq")
    bits = []
    while (1 << len(bits)) < count:
        bits.append(1 << len(bits))
    held = sums
    start = 0
    gathered = static_rows[None]
    for bit in bits:
        last = bit == bits[-1]
        up = (me & bit) != 0
        half = held.shape[0] // 2
        stat_rows = pack_stats(highest, total, width)
        if last:
            keep, give = held, held
        else:
            low, high = held[:half], held[half:]
            keep = jnp.where(up, high, low)
            give = jnp.where(up, low, high)
            start = start + jnp.where(up, half, 0)
        pieces = [give.astype(jnp.bfloat16), stat_rows] + ([static_rows] if last else [])
        got = swap(jnp.concatenate(pieces, axis=0), bit)
        rows = give.shape[0]
        theirs = unpack_stats(got[rows : rows + stat_rows.shape[0]], slot_total)
        highest, total, scale_a, scale_b = merge((highest, total), theirs)
        mine_a = lax.dynamic_slice_in_dim(scale_a, start, rows)[:, None]
        mine_b = lax.dynamic_slice_in_dim(scale_b, start, rows)[:, None]
        held = keep.astype(jnp.float32) * mine_a + got[:rows].astype(jnp.float32) * mine_b
        if last:
            other = got[rows + stat_rows.shape[0] :]
            gathered = jnp.stack(
                [jnp.where(up, other, static_rows), jnp.where(up, static_rows, other)]
            )
    held = held.astype(jnp.bfloat16)
    for bit in bits[-2::-1]:
        up = (me & bit) != 0
        rows = held.shape[0]
        got = swap(
            jnp.concatenate([held, gathered.reshape(-1, width)], axis=0), bit
        )
        held = jnp.concatenate(
            [jnp.where(up, got[:rows], held), jnp.where(up, held, got[:rows])], axis=0
        )
        other = got[rows:].reshape(gathered.shape)
        gathered = jnp.stack(
            [jnp.where(up, other, gathered), jnp.where(up, gathered, other)], axis=1
        ).reshape((-1,) + static_rows.shape)
    return highest, total, held, gathered


def on_device(
    tokens, out_grad, saved_logits, slot_params, slot_inputs, slot_outputs, expert_in, expert_out
):
    clip_count = lax.axis_size("clip")
    seq_count = lax.axis_size("seq")
    tok_feats = tokens[0]
    out_cot = out_grad[0]
    scores = saved_logits[0].astype(jnp.float32)
    width = tok_feats.shape[1]
    slot_total = scores.shape[1]
    clip_total = slot_inputs.shape[0]
    local_slots = slot_inputs.shape[1]
    expert_block = expert_in.shape[0]
    slot_each = local_slots // expert_block
    combine = jax.nn.softmax(scores, axis=1)
    partial_cot = jnp.einsum(
        "ts,td->sd", combine.astype(jnp.bfloat16), out_cot, preferred_element_type=jnp.float32
    )
    blocks = partial_cot.astype(jnp.bfloat16).reshape(
        clip_count * seq_count, local_slots, width
    )
    received = lax.all_to_all(blocks, BOTH, split_axis=0, concat_axis=0, tiled=True)
    local_max = jnp.max(scores, axis=0)
    raised = jnp.exp(scores - local_max)
    local_sum = jnp.sum(raised, axis=0)
    local_tok = jnp.einsum(
        "ts,td->sd", raised.astype(jnp.bfloat16), tok_feats, preferred_element_type=jnp.float32
    )
    seq_slots = slot_params.shape[1]
    static_rows = jnp.concatenate([slot_params.T, slot_outputs[0]], axis=0)
    col_max, col_sum, slot_tok, packed_all = seq_exchange(
        local_max, local_sum, local_tok, static_rows
    )
    param_all = packed_all[:, :seq_slots].reshape(slot_total, width)
    slot_out = packed_all[:, seq_slots:].reshape(slot_total, width)
    dispatch = raised * (jnp.exp(local_max - col_max) / col_sum)
    comb_cot = jnp.einsum("td,sd->ts", out_cot, slot_out, preferred_element_type=jnp.float32)
    comb_logit = combine * (comb_cot - jnp.sum(combine * comb_cot, axis=1, keepdims=True))
    expert_feed = slot_inputs.reshape(clip_total, expert_block, slot_each, width)
    hidden = jnp.einsum(
        "cejd,edh->cejh", expert_feed, expert_in, preferred_element_type=jnp.float32
    )
    expert_cot = received.reshape(clip_count, seq_count, expert_block, slot_each, width)
    expert_cot = jnp.sum(expert_cot.astype(jnp.float32), axis=1).astype(jnp.bfloat16)
    act_cot = jnp.einsum(
        "cejd,ehd->cejh", expert_cot, expert_out, preferred_element_type=jnp.float32
    )
    unused, pull_back = jax.vjp(jax.nn.gelu, hidden)
    hidden_cot = pull_back(act_cot)[0].astype(jnp.bfloat16)
    local_grad = jnp.einsum(
        "cejh,edh->cejd", hidden_cot, expert_in, preferred_element_type=jnp.float32
    ).astype(jnp.bfloat16)
    local_grad = local_grad.reshape(clip_count, 1, local_slots, width)
    copies = jnp.broadcast_to(local_grad, (clip_count, seq_count, local_slots, width))
    slot_grad = lax.all_to_all(
        copies.reshape(clip_count * seq_count, local_slots, width),
        BOTH,
        split_axis=0,
        concat_axis=0,
        tiled=True,
    ).reshape(slot_total, width)
    dispatch_b = dispatch.astype(jnp.bfloat16)
    disp_cot = jnp.einsum("td,sd->ts", tok_feats, slot_grad, preferred_element_type=jnp.float32)
    slot_dots = jnp.sum(slot_grad.astype(jnp.float32) * slot_tok.astype(jnp.float32), axis=1)
    slot_dots = slot_dots / col_sum
    disp_logit = dispatch * (disp_cot - slot_dots)
    logit_grad = (comb_logit + disp_logit).astype(jnp.bfloat16)
    both_weights = jnp.concatenate([dispatch_b, logit_grad], axis=1)
    both_rows = jnp.concatenate([slot_grad, param_all], axis=0)
    token_grad = jnp.dot(both_weights, both_rows, preferred_element_type=jnp.float32)
    return token_grad.astype(jnp.bfloat16)[None]


def solution(mesh):
    placed = (
        P("clip", "seq", None),
        P("clip", "seq", None),
        P("clip", "seq", None),
        P(None, "seq"),
        P(None, BOTH, None),
        P("clip", "seq", None),
        P(BOTH, None, None),
        P(BOTH, None, None),
    )
    return jax.shard_map(
        on_device, mesh=mesh, in_specs=placed, out_specs=P("clip", "seq", None), check_vma=False
    )
```

```python
import functools
import math
import jax
import jax.numpy as jnp
from jax import lax
from jax.experimental import pallas as pl
from jax.experimental.pallas import tpu as pltpu
from jax.sharding import PartitionSpec as P

BOTH = ("clip", "seq")
WHOLE = pl.BlockSpec(memory_space=pltpu.VMEM)
PLACED = pl.BlockSpec(memory_space=pl.ANY)
STAYS = pl.BlockSpec(memory_space=pltpu.HBM)
GROUP = 128
MIB = 1 << 20
FREE = pl.CostEstimate(flops=0, bytes_accessed=0, transcendentals=0)


def dot_nn(a, b):
    return jnp.dot(a, b, preferred_element_type=jnp.float32)


def dot_nt(a, b):
    return lax.dot_general(a, b, (((1,), (1,)), ((), ())), preferred_element_type=jnp.float32)


def dot_tn(a, b):
    return lax.dot_general(a, b, (((0,), (0,)), ((), ())), preferred_element_type=jnp.float32)


def fold_of(rows):
    return max(1, 8 // rows)


def pick(part, rows, fold, count):
    wide = fold * count
    row = lax.broadcasted_iota(jnp.int32, (wide, count), 0)
    col = lax.broadcasted_iota(jnp.int32, (wide, count), 1)
    span = fold * rows
    inner = lax.rem(row, span) - part * rows
    base = lax.div(row, span) * rows
    hit = (inner >= 0) & (inner < rows) & (col == base + inner)
    return jnp.where(hit, 1.0, 0.0).astype(jnp.bfloat16)


def fold_rows(value, rows, fold):
    if fold == 1:
        return value
    lanes = value.shape[1] // fold
    count = min(value.shape[0], GROUP)
    picks = [pick(part, rows, fold, count) for part in range(fold)]
    groups = []
    for at in range(0, value.shape[0], count):
        groups.append(
            sum(
                dot_nn(picks[part], value[at : at + count, part * lanes : (part + 1) * lanes])
                for part in range(fold)
            )
        )
    return jnp.concatenate(groups, axis=0).astype(jnp.bfloat16)


def unfold_rows(value, rows, fold):
    if fold == 1:
        return value
    count = min(value.shape[0] // fold, GROUP)
    picks = [pick(part, rows, fold, count) for part in range(fold)]
    groups = []
    for at in range(0, value.shape[0], fold * count):
        piece = value[at : at + fold * count]
        groups.append(
            jnp.concatenate([dot_tn(picks[part], piece) for part in range(fold)], axis=1)
        )
    return jnp.concatenate(groups, axis=0).astype(jnp.bfloat16)


def fetch(pairs, sems):
    copies = [
        pltpu.make_async_copy(source, held, sems.at[at]) for at, (source, held) in enumerate(pairs)
    ]
    for copy in copies:
        copy.start()
    return copies


def cot_kernel(rows, fold, logit_hbm, grad_hbm, out_ref, logit_ref, grad_ref, sems):
    got_logits, got_grad = fetch([(logit_hbm, logit_ref), (grad_hbm, grad_ref)], sems)
    got_logits.wait()
    scores = logit_ref[...].astype(jnp.float32)
    raised = jnp.exp(scores - jnp.max(scores, axis=1, keepdims=True))
    combine = raised / jnp.sum(raised, axis=1, keepdims=True)
    got_grad.wait()
    cot = dot_tn(combine.astype(jnp.bfloat16), grad_ref[...]).astype(jnp.bfloat16)
    out_ref[...] = fold_rows(cot, rows, fold)


def expert_kernel(
    clips, seqs, rows, fold, parts, got_ref, slope_ref, in_hbm, out_hbm, send_ref, in_ref, out_ref, sems
):
    span, lanes = fold * rows, got_ref.shape[1]
    hid = in_hbm.shape[1]
    chunk = hid // parts
    places = [pl.ds(part * chunk, chunk) for part in range(parts)]
    copies = [
        (
            pltpu.make_async_copy(out_hbm.at[at, :], out_ref.at[at, :], sems.at[0, part]),
            pltpu.make_async_copy(in_hbm.at[:, at], in_ref.at[:, at], sems.at[1, part]),
        )
        for part, at in enumerate(places)
    ]
    for pair in copies:
        for copy in pair:
            copy.start()
    got = got_ref[...].astype(jnp.float32).reshape(clips, seqs, span, lanes)
    cot = jnp.sum(got, axis=1).reshape(clips * span, lanes).astype(jnp.bfloat16)
    cot = unfold_rows(cot, rows, fold)
    grad = 0.0
    for pair, at in zip(copies, places):
        pair[0].wait()
        act_cot = dot_nt(cot, out_ref[at, :])
        hidden_cot = (act_cot * slope_ref[:, at]).astype(jnp.bfloat16)
        pair[1].wait()
        grad += dot_nt(hidden_cot, in_ref[:, at])
    grad = fold_rows(grad.astype(jnp.bfloat16), rows, fold).reshape(clips, 1, span, lanes)
    grad = jnp.broadcast_to(grad, (clips, seqs, span, lanes))
    send_ref[...] = grad.reshape(clips * seqs * span, lanes)


def token_kernel(
    rows, fold, chunk, tok_ref, got_ref, sum_ref, disp_ref, comb_ref, param_ref,
    out_hbm, stage, sems
):
    slot_grad = unfold_rows(got_ref[...], rows, fold)
    slots = slot_grad.shape[0]
    cross = dot_nt(sum_ref[...], slot_grad)
    row = lax.broadcasted_iota(jnp.int32, (slots, slots), 0)
    col = lax.broadcasted_iota(jnp.int32, (slots, slots), 1)
    slot_dots = jnp.sum(jnp.where(row == col, cross, 0.0), axis=0, keepdims=True)
    both_rows = jnp.concatenate([slot_grad, param_ref[...]], axis=0)
    copies = []
    for step in range(tok_ref.shape[0] // chunk):
        part = pl.ds(step * chunk, chunk)
        dispatch = disp_ref[part, :]
        disp_cot = dot_nt(tok_ref[part, :], slot_grad)
        logit_grad = comb_ref[part, :] + dispatch * (disp_cot - slot_dots)
        weights = jnp.concatenate([dispatch, logit_grad], axis=1).astype(jnp.bfloat16)
        stage[part, :] = dot_nn(weights, both_rows).astype(jnp.bfloat16)
        copy = pltpu.make_async_copy(stage.at[part, :], out_hbm.at[part, :], sems.at[step])
        copy.start()
        copies.append(copy)
    for copy in copies:
        copy.wait()


def stays(value):
    return pltpu.with_memory_space_constraint(value, pltpu.HBM)


def after(value, token):
    return lax.optimization_barrier((value, token))[0]


def seq_bits():
    count = lax.axis_size("seq")
    return [1 << place for place in reversed(range(count.bit_length() - 1))]


def swap(value, bit):
    count = lax.axis_size("seq")
    return lax.ppermute(value, "seq", [(i, i ^ bit) for i in range(count)])


def stat_places(slots, width):
    groups, per_row = slots // GROUP, width // GROUP
    return [
        [(g * GROUP, (v * groups + g) // per_row, (v * groups + g) % per_row * GROUP) for g in range(groups)]
        for v in range(4)
    ]


def stat_rows(slots, width):
    return -(-4 * slots // (16 * width)) * 16


def side_kernel(
    parts, logit_hbm, tok_hbm, param_hbm, slot_hbm, feed_ref, in_hbm,
    pack_ref, slope_ref, logit_ref, tok_ref, stat_ref, in_ref, sems
):
    slots, width = logit_ref.shape[1], tok_ref.shape[1]
    seq_slots = slot_hbm.shape[0]
    hid = in_hbm.shape[1]
    places = [pl.ds(part * (hid // parts), hid // parts) for part in range(parts)]
    copies = fetch(
        [
            (logit_hbm, logit_ref),
            (tok_hbm, tok_ref),
            (param_hbm, pack_ref.at[pl.ds(slots, seq_slots)]),
            (slot_hbm, pack_ref.at[pl.ds(slots + seq_slots, seq_slots)]),
        ]
        + [(in_hbm.at[:, at], in_ref.at[:, at]) for at in places],
        sems,
    )
    copies[0].wait()
    scores = logit_ref[...].astype(jnp.float32)
    highest = jnp.max(scores, axis=0, keepdims=True)
    raised = jnp.exp(scores - highest)
    total = jnp.sum(raised, axis=0, keepdims=True)
    part0 = total.astype(jnp.bfloat16).astype(jnp.float32)
    part1 = (total - part0).astype(jnp.bfloat16).astype(jnp.float32)
    part2 = total - part0 - part1
    stat_ref[...] = jnp.zeros_like(stat_ref)
    for vector, spots in zip((highest, part0, part1, part2), stat_places(slots, width)):
        for slot, row, lane in spots:
            stat_ref[row : row + 1, lane : lane + GROUP] = vector[:, slot : slot + GROUP]
    pack_ref[slots + 2 * seq_slots :] = stat_ref[...].astype(jnp.bfloat16)
    copies[1].wait()
    pack_ref[:slots] = dot_tn(raised.astype(jnp.bfloat16), tok_ref[...]).astype(jnp.bfloat16)
    feed = [feed_ref[clip].astype(jnp.float32) for clip in range(feed_ref.shape[0])]
    feed = jnp.concatenate(feed, axis=0).astype(jnp.bfloat16)
    root = math.sqrt(2.0 / math.pi)
    for at, copy in zip(places, copies[4:]):
        copy.wait()
        x = dot_nn(feed, in_ref[:, at])
        bend = jnp.tanh(root * (x + 0.044715 * (x * x * x)))
        grown = root * (1.0 + 3.0 * 0.044715 * (x * x))
        slope_ref[:, at] = 0.5 * (1.0 + bend) + 0.5 * x * (1.0 - bend * bend) * grown
    copies[2].wait()
    copies[3].wait()


def weight_kernel(seqs, me_ref, logit_hbm, grad_hbm, *refs):
    packs, (disp_ref, comb_ref, sum_ref, param_ref) = refs[:seqs], refs[seqs + 1 : seqs + 5]
    slot_ref, logit_ref, grad_ref, sems = refs[seqs + 5 :]
    slots, width = logit_ref.shape[1], grad_ref.shape[1]
    got_logits, got_grad = fetch([(logit_hbm, logit_ref), (grad_hbm, grad_ref)], sems)
    seq_slots = slots // seqs
    me = me_ref[0]
    stats = []
    for other, pack in enumerate(packs):
        base = slots + 2 * seq_slots
        rows = pack[base : base + stat_rows(slots, width)].astype(jnp.float32)
        parts = [
            jnp.concatenate([rows[r : r + 1, lane : lane + GROUP] for _, r, lane in places], axis=1)
            for places in stat_places(slots, width)
        ]
        stats.append((parts[0], parts[1] + parts[2] + parts[3]))
        at = pl.ds(pl.multiple_of((me ^ other) * seq_slots, seq_slots), seq_slots)
        param_ref[at, :] = pack[slots : slots + seq_slots]
        slot_ref[at, :] = pack[slots + seq_slots : slots + 2 * seq_slots]
    highest = functools.reduce(jnp.maximum, [top for top, _ in stats])
    total = sum(part * jnp.exp(top - highest) for top, part in stats)
    row = lax.broadcasted_iota(jnp.int32, (slots, slots), 0)
    col = lax.broadcasted_iota(jnp.int32, (slots, slots), 1)
    token_sum = jnp.zeros((slots, width), jnp.float32)
    for pack, (top, _) in zip(packs, stats):
        share = jnp.exp(top - highest) / total
        share = jnp.sum(jnp.where(row == col, share, 0.0), axis=1, keepdims=True)
        token_sum += share * pack[:slots].astype(jnp.float32)
    sum_ref[...] = token_sum.astype(jnp.bfloat16)
    got_logits.wait()
    scores = logit_ref[...].astype(jnp.float32)
    disp_ref[...] = jnp.exp(scores - highest) / total
    raised = jnp.exp(scores - jnp.max(scores, axis=1, keepdims=True))
    combine = raised / jnp.sum(raised, axis=1, keepdims=True)
    got_grad.wait()
    comb_cot = dot_nt(grad_ref[...], slot_ref[...])
    comb_ref[...] = combine * (comb_cot - jnp.sum(combine * comb_cot, axis=1, keepdims=True))


def on_device(
    tokens, out_grad, saved_logits, slot_params, slot_inputs, slot_outputs, expert_in, expert_out
):
    clip_count = lax.axis_size("clip")
    seq_count = lax.axis_size("seq")
    device_count = clip_count * seq_count
    tok_feats, out_cot, logit_raw = tokens[0], out_grad[0], saved_logits[0]
    token_total, width = tok_feats.shape
    slot_total = logit_raw.shape[1]
    clip_total, local_slots = slot_inputs.shape[:2]
    hid = expert_in.shape[2]
    fold = fold_of(local_slots)
    span, lanes = fold * local_slots, width // fold
    feed_rows = clip_total * local_slots
    f32, b16 = jnp.float32, jnp.bfloat16

    still_logits, still_grad = stays(logit_raw), stays(out_cot)
    blocks = pl.pallas_call(
        functools.partial(cot_kernel, local_slots, fold),
        out_shape=jax.ShapeDtypeStruct((device_count * span, lanes), b16),
        in_specs=[STAYS, STAYS],
        out_specs=WHOLE,
        scratch_shapes=[
            pltpu.VMEM((token_total, slot_total), b16),
            pltpu.VMEM((token_total, width), b16),
            pltpu.SemaphoreType.DMA((2,)),
        ],
        compiler_params=pltpu.CompilerParams(vmem_limit_bytes=16 * MIB),
        cost_estimate=FREE,
    )(still_logits, still_grad)
    received = lax.all_to_all(
        blocks.reshape(device_count, span, lanes), BOTH, split_axis=0, concat_axis=0, tiled=True
    )

    parts = math.gcd(hid // GROUP, 4)
    seq_slots = slot_params.shape[1]
    pack_rows = slot_total + 2 * seq_slots + stat_rows(slot_total, width)
    own, slope = pl.pallas_call(
        functools.partial(side_kernel, parts),
        out_shape=(
            jax.ShapeDtypeStruct((pack_rows, width), b16),
            jax.ShapeDtypeStruct((feed_rows, hid), f32),
        ),
        in_specs=[STAYS] * 4 + [WHOLE, STAYS],
        out_specs=(WHOLE, WHOLE),
        scratch_shapes=[
            pltpu.VMEM((token_total, slot_total), b16),
            pltpu.VMEM((token_total, width), b16),
            pltpu.VMEM((stat_rows(slot_total, width), width), f32),
            pltpu.VMEM((width, hid), b16),
            pltpu.SemaphoreType.DMA((4 + parts,)),
        ],
        compiler_params=pltpu.CompilerParams(vmem_limit_bytes=24 * MIB),
        cost_estimate=FREE,
    )(
        still_logits,
        stays(tok_feats),
        stays(slot_params.T),
        stays(slot_outputs[0]),
        slot_inputs,
        stays(expert_in[0]),
    )

    send = pl.pallas_call(
        functools.partial(expert_kernel, clip_count, seq_count, local_slots, fold, parts),
        out_shape=jax.ShapeDtypeStruct((device_count * span, lanes), b16),
        in_specs=[WHOLE, WHOLE, STAYS, STAYS],
        out_specs=WHOLE,
        scratch_shapes=[
            pltpu.VMEM((width, hid), b16),
            pltpu.VMEM((hid, width), b16),
            pltpu.SemaphoreType.DMA((2, parts)),
        ],
        compiler_params=pltpu.CompilerParams(vmem_limit_bytes=20 * MIB),
        cost_estimate=pl.CostEstimate(
            flops=4 * feed_rows * width * hid,
            bytes_accessed=4 * width * hid,
            transcendentals=0,
        ),
    )(received.reshape(device_count * span, lanes), slope, stays(expert_in[0]), stays(expert_out[0]))
    returned = lax.all_to_all(
        send.reshape(device_count, span, lanes), BOTH, split_axis=0, concat_axis=0, tiled=True
    )

    held = {0: own}
    for bit in seq_bits():
        for other in list(held):
            held[other ^ bit] = swap(held[other] if other == 0 else after(held[other], send), bit)
    dispatch, comb_logit, token_sum, param_all = pl.pallas_call(
        functools.partial(weight_kernel, seq_count),
        out_shape=(
            jax.ShapeDtypeStruct((token_total, slot_total), f32),
            jax.ShapeDtypeStruct((token_total, slot_total), f32),
            jax.ShapeDtypeStruct((slot_total, width), b16),
            jax.ShapeDtypeStruct((slot_total, width), b16),
        ),
        in_specs=[pl.BlockSpec(memory_space=pltpu.SMEM), STAYS, STAYS] + [WHOLE] * seq_count + [PLACED],
        out_specs=(WHOLE,) * 4,
        scratch_shapes=[
            pltpu.VMEM((slot_total, width), b16),
            pltpu.VMEM((token_total, slot_total), b16),
            pltpu.VMEM((token_total, width), b16),
            pltpu.SemaphoreType.DMA((2,)),
        ],
        compiler_params=pltpu.CompilerParams(vmem_limit_bytes=32 * MIB),
        cost_estimate=FREE,
    )(
        lax.axis_index("seq")[None],
        still_logits,
        still_grad,
        *[held[other] for other in range(seq_count)],
        send,
    )

    chunk = math.gcd(token_total, 128)
    token_grad = pl.pallas_call(
        functools.partial(token_kernel, local_slots, fold, chunk),
        out_shape=jax.ShapeDtypeStruct((token_total, width), b16),
        in_specs=[WHOLE] * 6,
        out_specs=PLACED,
        scratch_shapes=[
            pltpu.VMEM((token_total, width), b16),
            pltpu.SemaphoreType.DMA((token_total // chunk,)),
        ],
        compiler_params=pltpu.CompilerParams(vmem_limit_bytes=16 * MIB),
        cost_estimate=pl.CostEstimate(
            flops=6 * token_total * width * slot_total,
            bytes_accessed=4 * token_total * width,
            transcendentals=0,
        ),
    )(
        tok_feats,
        returned.reshape(device_count * span, lanes),
        token_sum,
        dispatch,
        comb_logit,
        param_all,
    )
    return token_grad[None]


def solution(mesh):
    placed = (
        P("clip", "seq", None),
        P("clip", "seq", None),
        P("clip", "seq", None),
        P(None, "seq"),
        P(None, BOTH, None),
        P("clip", "seq", None),
        P(BOTH, None, None),
        P(BOTH, None, None),
    )
    return jax.shard_map(
        on_device, mesh=mesh, in_specs=placed, out_specs=P("clip", "seq", None), check_vma=False
    )
```

```python
import functools
import math
import jax
import jax.numpy as jnp
from jax import lax
from jax.experimental import pallas as pl
from jax.experimental.pallas import tpu as pltpu
from jax.sharding import PartitionSpec as P

BOTH = ("clip", "seq")
ROUND = ("seq", "clip")
WHOLE = pl.BlockSpec(memory_space=pltpu.VMEM)
PLACED = pl.BlockSpec(memory_space=pl.ANY)
STAYS = pl.BlockSpec(memory_space=pltpu.HBM)
GROUP = 128
MIB = 1 << 20
FREE = pl.CostEstimate(flops=0, bytes_accessed=0, transcendentals=0)


def dot_nn(a, b):
    return jnp.dot(a, b, preferred_element_type=jnp.float32)


def dot_nt(a, b):
    return lax.dot_general(a, b, (((1,), (1,)), ((), ())), preferred_element_type=jnp.float32)


def dot_tn(a, b):
    return lax.dot_general(a, b, (((0,), (0,)), ((), ())), preferred_element_type=jnp.float32)


def fetch(pairs, sems):
    copies = [
        pltpu.make_async_copy(source, held, sems.at[at]) for at, (source, held) in enumerate(pairs)
    ]
    for copy in copies:
        copy.start()
    return copies


def cot_kernel(seqs, logit_hbm, grad_hbm, out_ref, logit_ref, grad_ref, sems):
    got_logits, got_grad = fetch([(logit_hbm, logit_ref), (grad_hbm, grad_ref)], sems)
    got_logits.wait()
    scores = logit_ref[...].astype(jnp.float32)
    raised = jnp.exp(scores - jnp.max(scores, axis=1, keepdims=True))
    combine = raised / jnp.sum(raised, axis=1, keepdims=True)
    got_grad.wait()
    cot = dot_tn(combine.astype(jnp.bfloat16), grad_ref[...])
    devices, rows, width = out_ref.shape
    cot = cot.reshape(devices // seqs, seqs, rows, width).swapaxes(0, 1)
    out_ref[...] = cot.reshape(out_ref.shape).astype(jnp.bfloat16)


def expert_kernel(
    clips, seqs, got_ref, slope_ref, kept_ref, in_hbm, out_hbm, send_ref, in_ref, out_ref, cot_ref, sems
):
    rows, width = got_ref.shape[1:]
    hid, chunk = in_hbm.shape[1], kept_ref.shape[0]
    parts = hid // chunk

    def place(part):
        return pl.ds(pl.multiple_of(part * chunk, chunk), chunk)

    def out_copy(part):
        return pltpu.make_async_copy(
            out_hbm.at[place(part), :], out_ref.at[place(part - 1), :], sems.at[part - 1]
        )

    def in_copy(part):
        at = place(part)
        return pltpu.make_async_copy(in_hbm.at[:, at], in_ref.at[:, at], sems.at[parts - 1 + part])

    for part in range(1, parts):
        out_copy(part).start()
    for part in range(parts):
        in_copy(part).start()
    got = got_ref[...].astype(jnp.float32).reshape(seqs, clips, rows, width)
    cot = jnp.sum(got, axis=0).reshape(clips * rows, width).astype(jnp.bfloat16)
    first = dot_nt(cot, kept_ref[...]) * slope_ref[:, :chunk]
    cot_ref[:, :chunk] = first.astype(jnp.bfloat16)

    @pl.loop(1, parts)
    def _(part):
        out_copy(part).wait()
        at = place(part)
        act_cot = dot_nt(cot, out_ref[place(part - 1), :])
        cot_ref[:, at] = (act_cot * slope_ref[:, at]).astype(jnp.bfloat16)

    def add(part, total):
        in_copy(part).wait()
        at = place(part)
        return total + dot_nt(cot_ref[:, at], in_ref[:, at])

    grad = lax.fori_loop(0, parts, add, jnp.zeros((clips * rows, width), jnp.float32))
    grad = grad.reshape(1, clips, rows, width)
    grad = jnp.broadcast_to(grad, (seqs, clips, rows, width))
    send_ref[...] = grad.reshape(send_ref.shape).astype(jnp.bfloat16)


def token_kernel(
    seqs, chunk, tok_ref, got_ref, sum_ref, disp_ref, comb_ref, param_ref,
    out_hbm, stage, sems
):
    slots, width = param_ref.shape
    devices, rows = got_ref.shape[:2]
    slot_grad = got_ref[...].astype(jnp.float32).reshape(seqs, devices // seqs, rows, width)
    slot_grad = slot_grad.swapaxes(0, 1).reshape(slots, width).astype(jnp.bfloat16)
    cross = dot_nt(sum_ref[...], slot_grad)
    row = lax.broadcasted_iota(jnp.int32, (slots, slots), 0)
    col = lax.broadcasted_iota(jnp.int32, (slots, slots), 1)
    slot_dots = jnp.sum(jnp.where(row == col, cross, 0.0), axis=0, keepdims=True)
    both_rows = jnp.concatenate([slot_grad, param_ref[...]], axis=0)
    copies = []
    for step in range(tok_ref.shape[0] // chunk):
        part = pl.ds(step * chunk, chunk)
        dispatch = disp_ref[part, :]
        disp_cot = dot_nt(tok_ref[part, :], slot_grad)
        logit_grad = comb_ref[part, :] + dispatch * (disp_cot - slot_dots)
        weights = jnp.concatenate([dispatch, logit_grad], axis=1).astype(jnp.bfloat16)
        stage[part, :] = dot_nn(weights, both_rows).astype(jnp.bfloat16)
        copy = pltpu.make_async_copy(stage.at[part, :], out_hbm.at[part, :], sems.at[step])
        copy.start()
        copies.append(copy)
    for copy in copies:
        copy.wait()


def stays(value):
    return pltpu.with_memory_space_constraint(value, pltpu.HBM)


def after(value, token):
    return lax.optimization_barrier((value, token))[0]


def seq_bits():
    count = lax.axis_size("seq")
    return [1 << place for place in reversed(range(count.bit_length() - 1))]


def swap(value, bit):
    count = lax.axis_size("seq")
    return lax.ppermute(value, "seq", [(i, i ^ bit) for i in range(count)])


def stat_places(slots, width):
    groups, per_row = slots // GROUP, width // GROUP
    return [
        [(g * GROUP, (v * groups + g) // per_row, (v * groups + g) % per_row * GROUP) for g in range(groups)]
        for v in range(4)
    ]


def stat_rows(slots, width):
    return -(-4 * slots // (16 * width)) * 16


def side_kernel(
    parts, logit_hbm, tok_hbm, param_hbm, slot_hbm, feed_hbm, in_hbm, out_hbm,
    pack_ref, slope_ref, kept_ref, logit_ref, tok_ref, feed_ref, stat_ref, in_ref, sems
):
    slots, width = logit_ref.shape[1], tok_ref.shape[1]
    seq_slots = slot_hbm.shape[0]
    hid = in_hbm.shape[1]
    places = [pl.ds(part * (hid // parts), hid // parts) for part in range(parts)]
    copies = fetch(
        [
            (logit_hbm, logit_ref),
            (tok_hbm, tok_ref),
            (param_hbm, pack_ref.at[pl.ds(slots, seq_slots)]),
            (slot_hbm, pack_ref.at[pl.ds(slots + seq_slots, seq_slots)]),
            (feed_hbm, feed_ref),
        ]
        + [(in_hbm.at[:, at], in_ref.at[:, at]) for at in places]
        + [(out_hbm.at[pl.ds(0, kept_ref.shape[0])], kept_ref)],
        sems,
    )
    copies[0].wait()
    scores = logit_ref[...].astype(jnp.float32)
    highest = jnp.max(scores, axis=0, keepdims=True)
    raised = jnp.exp(scores - highest)
    total = jnp.sum(raised, axis=0, keepdims=True)
    part0 = total.astype(jnp.bfloat16).astype(jnp.float32)
    part1 = (total - part0).astype(jnp.bfloat16).astype(jnp.float32)
    part2 = total - part0 - part1
    stat_ref[...] = jnp.zeros_like(stat_ref)
    for vector, spots in zip((highest, part0, part1, part2), stat_places(slots, width)):
        for slot, row, lane in spots:
            stat_ref[row : row + 1, lane : lane + GROUP] = vector[:, slot : slot + GROUP]
    pack_ref[slots + 2 * seq_slots :] = stat_ref[...].astype(jnp.bfloat16)
    copies[1].wait()
    pack_ref[:slots] = dot_tn(raised.astype(jnp.bfloat16), tok_ref[...]).astype(jnp.bfloat16)
    copies[4].wait()
    feed = [feed_ref[clip].astype(jnp.float32) for clip in range(feed_ref.shape[0])]
    feed = jnp.concatenate(feed, axis=0).astype(jnp.bfloat16)
    root = math.sqrt(2.0 / math.pi)
    for at, copy in zip(places, copies[5:]):
        copy.wait()
        x = dot_nn(feed, in_ref[:, at])
        bend = jnp.tanh(root * (x + 0.044715 * (x * x * x)))
        grown = root * (1.0 + 3.0 * 0.044715 * (x * x))
        slope_ref[:, at] = 0.5 * (1.0 + bend) + 0.5 * x * (1.0 - bend * bend) * grown
    copies[2].wait()
    copies[3].wait()
    copies[-1].wait()


def weight_kernel(seqs, me_ref, logit_hbm, grad_hbm, *refs):
    packs, (disp_ref, comb_ref, sum_ref, param_ref) = refs[:seqs], refs[seqs + 1 : seqs + 5]
    slot_ref, logit_ref, grad_ref, sems = refs[seqs + 5 :]
    slots, width = logit_ref.shape[1], grad_ref.shape[1]
    got_logits, got_grad = fetch([(logit_hbm, logit_ref), (grad_hbm, grad_ref)], sems)
    seq_slots = slots // seqs
    me = me_ref[0]
    stats = []
    for other, pack in enumerate(packs):
        base = slots + 2 * seq_slots
        rows = pack[base : base + stat_rows(slots, width)].astype(jnp.float32)
        parts = [
            jnp.concatenate([rows[r : r + 1, lane : lane + GROUP] for _, r, lane in places], axis=1)
            for places in stat_places(slots, width)
        ]
        stats.append((parts[0], parts[1] + parts[2] + parts[3]))
        at = pl.ds(pl.multiple_of((me ^ other) * seq_slots, seq_slots), seq_slots)
        param_ref[at, :] = pack[slots : slots + seq_slots]
        slot_ref[at, :] = pack[slots + seq_slots : slots + 2 * seq_slots]
    highest = functools.reduce(jnp.maximum, [top for top, _ in stats])
    total = sum(part * jnp.exp(top - highest) for top, part in stats)
    row = lax.broadcasted_iota(jnp.int32, (slots, slots), 0)
    col = lax.broadcasted_iota(jnp.int32, (slots, slots), 1)
    token_sum = jnp.zeros((slots, width), jnp.float32)
    for pack, (top, _) in zip(packs, stats):
        share = jnp.exp(top - highest) / total
        share = jnp.sum(jnp.where(row == col, share, 0.0), axis=1, keepdims=True)
        token_sum += share * pack[:slots].astype(jnp.float32)
    sum_ref[...] = token_sum.astype(jnp.bfloat16)
    got_logits.wait()
    scores = logit_ref[...].astype(jnp.float32)
    disp_ref[...] = jnp.exp(scores - highest) / total
    raised = jnp.exp(scores - jnp.max(scores, axis=1, keepdims=True))
    combine = raised / jnp.sum(raised, axis=1, keepdims=True)
    got_grad.wait()
    comb_cot = dot_nt(grad_ref[...], slot_ref[...])
    comb_ref[...] = combine * (comb_cot - jnp.sum(combine * comb_cot, axis=1, keepdims=True))


def on_device(
    tokens, out_grad, saved_logits, slot_params, slot_inputs, slot_outputs, expert_in, expert_out
):
    clip_count = lax.axis_size("clip")
    seq_count = lax.axis_size("seq")
    device_count = clip_count * seq_count
    tok_feats, out_cot, logit_raw = tokens[0], out_grad[0], saved_logits[0]
    token_total, width = tok_feats.shape
    slot_total = logit_raw.shape[1]
    clip_total, local_slots = slot_inputs.shape[:2]
    hid = expert_in.shape[2]
    feed_rows = clip_total * local_slots
    f32, b16 = jnp.float32, jnp.bfloat16

    still_logits, still_grad = stays(logit_raw), stays(out_cot)
    still_in, still_out = stays(expert_in[0]), stays(expert_out[0])
    blocks = pl.pallas_call(
        functools.partial(cot_kernel, seq_count),
        out_shape=jax.ShapeDtypeStruct((device_count, local_slots, width), b16),
        in_specs=[STAYS, STAYS],
        out_specs=WHOLE,
        scratch_shapes=[
            pltpu.VMEM((token_total, slot_total), b16),
            pltpu.VMEM((token_total, width), b16),
            pltpu.SemaphoreType.DMA((2,)),
        ],
        compiler_params=pltpu.CompilerParams(vmem_limit_bytes=16 * MIB),
        cost_estimate=FREE,
    )(still_logits, still_grad)
    received = lax.all_to_all(blocks, ROUND, split_axis=0, concat_axis=0, tiled=True)

    parts = math.gcd(hid // GROUP, 4)
    seq_slots = slot_params.shape[1]
    pack_rows = slot_total + 2 * seq_slots + stat_rows(slot_total, width)
    thirds = math.gcd(hid // GROUP, 3)
    kept_rows = hid // thirds if thirds > 1 else GROUP
    own, slope, kept = pl.pallas_call(
        functools.partial(side_kernel, parts),
        out_shape=(
            jax.ShapeDtypeStruct((pack_rows, width), b16),
            jax.ShapeDtypeStruct((feed_rows, hid), f32),
            pltpu.VMEM((kept_rows, width), b16),
        ),
        in_specs=[STAYS] * 7,
        out_specs=(WHOLE,) * 3,
        scratch_shapes=[
            pltpu.VMEM((token_total, slot_total), b16),
            pltpu.VMEM((token_total, width), b16),
            pltpu.VMEM(slot_inputs.shape, b16),
            pltpu.VMEM((stat_rows(slot_total, width), width), f32),
            pltpu.VMEM((width, hid), b16),
            pltpu.SemaphoreType.DMA((6 + parts,)),
        ],
        compiler_params=pltpu.CompilerParams(vmem_limit_bytes=24 * MIB),
        cost_estimate=FREE,
    )(
        still_logits,
        stays(tok_feats),
        stays(slot_params.T),
        stays(slot_outputs[0]),
        stays(slot_inputs),
        still_in,
        still_out,
    )

    send = pl.pallas_call(
        functools.partial(expert_kernel, clip_count, seq_count),
        out_shape=jax.ShapeDtypeStruct((device_count, local_slots, width), b16),
        in_specs=[WHOLE, WHOLE, WHOLE, STAYS, STAYS],
        out_specs=WHOLE,
        scratch_shapes=[
            pltpu.VMEM((width, hid), b16),
            pltpu.VMEM((hid - kept_rows, width), b16),
            pltpu.VMEM((feed_rows, hid), b16),
            pltpu.SemaphoreType.DMA((2 * (hid // kept_rows) - 1,)),
        ],
        compiler_params=pltpu.CompilerParams(vmem_limit_bytes=20 * MIB),
        cost_estimate=pl.CostEstimate(
            flops=4 * feed_rows * width * hid,
            bytes_accessed=4 * width * hid,
            transcendentals=0,
        ),
    )(
        received,
        slope,
        pltpu.with_memory_space_constraint(kept, pltpu.VMEM),
        still_in,
        still_out,
    )
    returned = lax.all_to_all(send, ROUND, split_axis=0, concat_axis=0, tiled=True)

    held = {0: own}
    for bit in seq_bits():
        for other in list(held):
            held[other ^ bit] = swap(held[other] if other == 0 else after(held[other], send), bit)
    dispatch, comb_logit, token_sum, param_all = pl.pallas_call(
        functools.partial(weight_kernel, seq_count),
        out_shape=(
            jax.ShapeDtypeStruct((token_total, slot_total), f32),
            jax.ShapeDtypeStruct((token_total, slot_total), f32),
            jax.ShapeDtypeStruct((slot_total, width), b16),
            jax.ShapeDtypeStruct((slot_total, width), b16),
        ),
        in_specs=[pl.BlockSpec(memory_space=pltpu.SMEM), STAYS, STAYS] + [WHOLE] * seq_count + [PLACED],
        out_specs=(WHOLE,) * 4,
        scratch_shapes=[
            pltpu.VMEM((slot_total, width), b16),
            pltpu.VMEM((token_total, slot_total), b16),
            pltpu.VMEM((token_total, width), b16),
            pltpu.SemaphoreType.DMA((2,)),
        ],
        compiler_params=pltpu.CompilerParams(vmem_limit_bytes=32 * MIB),
        cost_estimate=FREE,
    )(
        lax.axis_index("seq")[None],
        still_logits,
        still_grad,
        *[held[other] for other in range(seq_count)],
        send,
    )

    chunk = math.gcd(token_total, 128)
    token_grad = pl.pallas_call(
        functools.partial(token_kernel, seq_count, chunk),
        out_shape=jax.ShapeDtypeStruct((token_total, width), b16),
        in_specs=[WHOLE] * 6,
        out_specs=PLACED,
        scratch_shapes=[
            pltpu.VMEM((token_total, width), b16),
            pltpu.SemaphoreType.DMA((token_total // chunk,)),
        ],
        compiler_params=pltpu.CompilerParams(vmem_limit_bytes=16 * MIB),
        cost_estimate=pl.CostEstimate(
            flops=6 * token_total * width * slot_total,
            bytes_accessed=4 * token_total * width,
            transcendentals=0,
        ),
    )(
        tok_feats,
        returned,
        token_sum,
        dispatch,
        comb_logit,
        param_all,
    )
    return token_grad[None]


def solution(mesh):
    placed = (
        P("clip", "seq", None),
        P("clip", "seq", None),
        P("clip", "seq", None),
        P(None, "seq"),
        P(None, BOTH, None),
        P("clip", "seq", None),
        P(BOTH, None, None),
        P(BOTH, None, None),
    )
    return jax.shard_map(
        on_device, mesh=mesh, in_specs=placed, out_specs=P("clip", "seq", None), check_vma=False
    )
```

```python
import functools
import math
import jax
import jax.numpy as jnp
from jax import lax
from jax.experimental import pallas as pl
from jax.experimental.pallas import tpu as pltpu
from jax.sharding import PartitionSpec as P

BOTH = ("clip", "seq")
ROUND = ("seq", "clip")
WHOLE = pl.BlockSpec(memory_space=pltpu.VMEM)
PLACED = pl.BlockSpec(memory_space=pl.ANY)
STAYS = pl.BlockSpec(memory_space=pltpu.HBM)
GROUP = 128
MIB = 1 << 20
FREE = pl.CostEstimate(flops=0, bytes_accessed=0, transcendentals=0)


def dot_nn(a, b):
    return jnp.dot(a, b, preferred_element_type=jnp.float32)


def dot_nt(a, b):
    return lax.dot_general(a, b, (((1,), (1,)), ((), ())), preferred_element_type=jnp.float32)


def dot_tn(a, b):
    return lax.dot_general(a, b, (((0,), (0,)), ((), ())), preferred_element_type=jnp.float32)


def fetch(pairs, sems):
    copies = [
        pltpu.make_async_copy(source, held, sems.at[at]) for at, (source, held) in enumerate(pairs)
    ]
    for copy in copies:
        copy.start()
    return copies


def cot_kernel(seqs, logit_hbm, grad_hbm, out_ref, logit_ref, grad_ref, sems):
    got_logits, got_grad = fetch([(logit_hbm, logit_ref), (grad_hbm, grad_ref)], sems)
    got_logits.wait()
    scores = logit_ref[...].astype(jnp.float32)
    raised = jnp.exp(scores - jnp.max(scores, axis=1, keepdims=True))
    combine = raised / jnp.sum(raised, axis=1, keepdims=True)
    got_grad.wait()
    cot = dot_tn(combine.astype(jnp.bfloat16), grad_ref[...])
    devices, rows, width = out_ref.shape
    cot = cot.reshape(devices // seqs, seqs, rows, width).swapaxes(0, 1)
    out_ref[...] = cot.reshape(out_ref.shape).astype(jnp.bfloat16)


def expert_kernel(
    clips, seqs, chunk, wide, got_ref, kept_ref, slope_hbm, in_hbm, out_hbm, send_ref,
    slope_ref, in_ref, out_ref, act_ref, cot_ref, sems
):
    rows, width = got_ref.shape[1:]
    hid, kept = in_hbm.shape[1], kept_ref.shape[0]
    outs, ins = (hid - kept) // chunk, hid // wide

    def place(part, size, shift=0):
        return pl.ds(pl.multiple_of(shift + part * size, GROUP), size)

    def out_copy(part):
        return pltpu.make_async_copy(
            out_hbm.at[place(part, chunk, kept), :], out_ref.at[place(part, chunk), :], sems.at[part]
        )

    def in_copy(part):
        at = place(part, wide)
        return pltpu.make_async_copy(in_hbm.at[:, at], in_ref.at[:, at], sems.at[outs + part])

    slope_copy = pltpu.make_async_copy(slope_hbm, slope_ref, sems.at[outs + ins])
    slope_copy.start()
    for part in range(outs):
        out_copy(part).start()
    for part in range(ins):
        in_copy(part).start()
    got = got_ref[...].astype(jnp.float32).reshape(seqs, clips, rows, width)
    cot = jnp.sum(got, axis=0).reshape(clips * rows, width).astype(jnp.bfloat16)

    @pl.loop(0, kept // chunk)
    def _(part):
        at = place(part, chunk)
        act_ref[:, at] = dot_nt(cot, kept_ref[at, :])

    slope_copy.wait()
    cot_ref[:, :kept] = (act_ref[...] * slope_ref[:, :kept]).astype(jnp.bfloat16)

    @pl.loop(0, outs)
    def _(part):
        out_copy(part).wait()
        at = place(part, chunk, kept)
        act_cot = dot_nt(cot, out_ref[place(part, chunk), :])
        cot_ref[:, at] = (act_cot * slope_ref[:, at]).astype(jnp.bfloat16)

    def add(part, total):
        in_copy(part).wait()
        at = place(part, wide)
        return total + dot_nt(cot_ref[:, at], in_ref[:, at])

    grad = lax.fori_loop(0, ins, add, jnp.zeros((clips * rows, width), jnp.float32))
    grad = grad.reshape(1, clips, rows, width)
    grad = jnp.broadcast_to(grad, (seqs, clips, rows, width))
    send_ref[...] = grad.reshape(send_ref.shape).astype(jnp.bfloat16)


def token_kernel(
    seqs, chunk, tok_ref, got_ref, sum_ref, disp_ref, comb_ref, param_ref,
    out_hbm, stage, sems
):
    slots, width = param_ref.shape
    devices, rows = got_ref.shape[:2]
    slot_grad = got_ref[...].astype(jnp.float32).reshape(seqs, devices // seqs, rows, width)
    slot_grad = slot_grad.swapaxes(0, 1).reshape(slots, width).astype(jnp.bfloat16)
    cross = dot_nt(sum_ref[...], slot_grad)
    row = lax.broadcasted_iota(jnp.int32, (slots, slots), 0)
    col = lax.broadcasted_iota(jnp.int32, (slots, slots), 1)
    slot_dots = jnp.sum(jnp.where(row == col, cross, 0.0), axis=0, keepdims=True)
    both_rows = jnp.concatenate([slot_grad, param_ref[...]], axis=0)
    copies = []
    for step in range(tok_ref.shape[0] // chunk):
        part = pl.ds(step * chunk, chunk)
        dispatch = disp_ref[part, :]
        disp_cot = dot_nt(tok_ref[part, :], slot_grad)
        logit_grad = comb_ref[part, :] + dispatch * (disp_cot - slot_dots)
        weights = jnp.concatenate([dispatch, logit_grad], axis=1).astype(jnp.bfloat16)
        stage[part, :] = dot_nn(weights, both_rows).astype(jnp.bfloat16)
        copy = pltpu.make_async_copy(stage.at[part, :], out_hbm.at[part, :], sems.at[step])
        copy.start()
        copies.append(copy)
    for copy in copies:
        copy.wait()


def stays(value):
    return pltpu.with_memory_space_constraint(value, pltpu.HBM)


def after(value, token):
    return lax.optimization_barrier((value, token))[0]


def seq_bits():
    count = lax.axis_size("seq")
    return [1 << place for place in reversed(range(count.bit_length() - 1))]


def swap(value, bit):
    count = lax.axis_size("seq")
    return lax.ppermute(value, "seq", [(i, i ^ bit) for i in range(count)])


def stat_places(slots, width):
    groups, per_row = slots // GROUP, width // GROUP
    return [
        [(g * GROUP, (v * groups + g) // per_row, (v * groups + g) % per_row * GROUP) for g in range(groups)]
        for v in range(4)
    ]


def stat_rows(slots, width):
    return -(-4 * slots // (16 * width)) * 16


def side_kernel(
    parts, logit_hbm, tok_hbm, param_hbm, slot_hbm, feed_hbm, in_hbm, out_hbm,
    pack_ref, slope_ref, kept_ref, logit_ref, tok_ref, feed_ref, stat_ref, in_ref, sems
):
    slots, width = logit_ref.shape[1], tok_ref.shape[1]
    seq_slots = slot_hbm.shape[0]
    hid = in_hbm.shape[1]
    places = [pl.ds(part * (hid // parts), hid // parts) for part in range(parts)]
    copies = fetch(
        [
            (logit_hbm, logit_ref),
            (tok_hbm, tok_ref),
            (param_hbm, pack_ref.at[pl.ds(slots, seq_slots)]),
            (slot_hbm, pack_ref.at[pl.ds(slots + seq_slots, seq_slots)]),
            (feed_hbm, feed_ref),
        ]
        + [(in_hbm.at[:, at], in_ref.at[:, at]) for at in places]
        + [(out_hbm.at[pl.ds(0, kept_ref.shape[0])], kept_ref)],
        sems,
    )
    copies[0].wait()
    scores = logit_ref[...].astype(jnp.float32)
    highest = jnp.max(scores, axis=0, keepdims=True)
    raised = jnp.exp(scores - highest)
    total = jnp.sum(raised, axis=0, keepdims=True)
    part0 = total.astype(jnp.bfloat16).astype(jnp.float32)
    part1 = (total - part0).astype(jnp.bfloat16).astype(jnp.float32)
    part2 = total - part0 - part1
    stat_ref[...] = jnp.zeros_like(stat_ref)
    for vector, spots in zip((highest, part0, part1, part2), stat_places(slots, width)):
        for slot, row, lane in spots:
            stat_ref[row : row + 1, lane : lane + GROUP] = vector[:, slot : slot + GROUP]
    pack_ref[slots + 2 * seq_slots :] = stat_ref[...].astype(jnp.bfloat16)
    copies[1].wait()
    pack_ref[:slots] = dot_tn(raised.astype(jnp.bfloat16), tok_ref[...]).astype(jnp.bfloat16)
    copies[4].wait()
    feed = [feed_ref[clip].astype(jnp.float32) for clip in range(feed_ref.shape[0])]
    feed = jnp.concatenate(feed, axis=0).astype(jnp.bfloat16)
    root = math.sqrt(2.0 / math.pi)
    for at, copy in zip(places, copies[5:]):
        copy.wait()
        x = dot_nn(feed, in_ref[:, at])
        bend = jnp.tanh(root * (x + 0.044715 * (x * x * x)))
        grown = root * (1.0 + 3.0 * 0.044715 * (x * x))
        slope_ref[:, at] = 0.5 * (1.0 + bend) + 0.5 * x * (1.0 - bend * bend) * grown
    copies[2].wait()
    copies[3].wait()
    copies[-1].wait()


def weight_kernel(seqs, me_ref, logit_hbm, grad_hbm, *refs):
    packs, (disp_ref, comb_ref, sum_ref, param_ref) = refs[:seqs], refs[seqs + 1 : seqs + 5]
    slot_ref, logit_ref, grad_ref, sems = refs[seqs + 5 :]
    slots, width = logit_ref.shape[1], grad_ref.shape[1]
    got_logits, got_grad = fetch([(logit_hbm, logit_ref), (grad_hbm, grad_ref)], sems)
    seq_slots = slots // seqs
    me = me_ref[0]
    stats = []
    for other, pack in enumerate(packs):
        base = slots + 2 * seq_slots
        rows = pack[base : base + stat_rows(slots, width)].astype(jnp.float32)
        parts = [
            jnp.concatenate([rows[r : r + 1, lane : lane + GROUP] for _, r, lane in places], axis=1)
            for places in stat_places(slots, width)
        ]
        stats.append((parts[0], parts[1] + parts[2] + parts[3]))
        at = pl.ds(pl.multiple_of((me ^ other) * seq_slots, seq_slots), seq_slots)
        param_ref[at, :] = pack[slots : slots + seq_slots]
        slot_ref[at, :] = pack[slots + seq_slots : slots + 2 * seq_slots]
    highest = functools.reduce(jnp.maximum, [top for top, _ in stats])
    total = sum(part * jnp.exp(top - highest) for top, part in stats)
    row = lax.broadcasted_iota(jnp.int32, (slots, slots), 0)
    col = lax.broadcasted_iota(jnp.int32, (slots, slots), 1)
    token_sum = jnp.zeros((slots, width), jnp.float32)
    for pack, (top, _) in zip(packs, stats):
        share = jnp.exp(top - highest) / total
        share = jnp.sum(jnp.where(row == col, share, 0.0), axis=1, keepdims=True)
        token_sum += share * pack[:slots].astype(jnp.float32)
    sum_ref[...] = token_sum.astype(jnp.bfloat16)
    got_logits.wait()
    scores = logit_ref[...].astype(jnp.float32)
    disp_ref[...] = jnp.exp(scores - highest) / total
    raised = jnp.exp(scores - jnp.max(scores, axis=1, keepdims=True))
    combine = raised / jnp.sum(raised, axis=1, keepdims=True)
    got_grad.wait()
    comb_cot = dot_nt(grad_ref[...], slot_ref[...])
    comb_ref[...] = combine * (comb_cot - jnp.sum(combine * comb_cot, axis=1, keepdims=True))


def on_device(
    tokens, out_grad, saved_logits, slot_params, slot_inputs, slot_outputs, expert_in, expert_out
):
    clip_count = lax.axis_size("clip")
    seq_count = lax.axis_size("seq")
    device_count = clip_count * seq_count
    tok_feats, out_cot, logit_raw = tokens[0], out_grad[0], saved_logits[0]
    token_total, width = tok_feats.shape
    slot_total = logit_raw.shape[1]
    clip_total, local_slots = slot_inputs.shape[:2]
    hid = expert_in.shape[2]
    feed_rows = clip_total * local_slots
    f32, b16 = jnp.float32, jnp.bfloat16

    still_logits, still_grad = stays(logit_raw), stays(out_cot)
    still_in, still_out = stays(expert_in[0]), stays(expert_out[0])
    blocks = pl.pallas_call(
        functools.partial(cot_kernel, seq_count),
        out_shape=jax.ShapeDtypeStruct((device_count, local_slots, width), b16),
        in_specs=[STAYS, STAYS],
        out_specs=WHOLE,
        scratch_shapes=[
            pltpu.VMEM((token_total, slot_total), b16),
            pltpu.VMEM((token_total, width), b16),
            pltpu.SemaphoreType.DMA((2,)),
        ],
        compiler_params=pltpu.CompilerParams(vmem_limit_bytes=16 * MIB),
        cost_estimate=FREE,
    )(still_logits, still_grad)
    received = lax.all_to_all(blocks, ROUND, split_axis=0, concat_axis=0, tiled=True)

    parts = math.gcd(hid // GROUP, 4)
    seq_slots = slot_params.shape[1]
    pack_rows = slot_total + 2 * seq_slots + stat_rows(slot_total, width)
    pieces = math.gcd(hid // GROUP, 6)
    chunk, wide = hid // pieces, hid // math.gcd(pieces, 3)
    kept_rows = max(pieces // 2, 1) * chunk
    own, slope, kept = pl.pallas_call(
        functools.partial(side_kernel, parts),
        out_shape=(
            jax.ShapeDtypeStruct((pack_rows, width), b16),
            pltpu.HBM((feed_rows, hid), f32),
            pltpu.VMEM((kept_rows, width), b16),
        ),
        in_specs=[STAYS] * 7,
        out_specs=(WHOLE,) * 3,
        scratch_shapes=[
            pltpu.VMEM((token_total, slot_total), b16),
            pltpu.VMEM((token_total, width), b16),
            pltpu.VMEM(slot_inputs.shape, b16),
            pltpu.VMEM((stat_rows(slot_total, width), width), f32),
            pltpu.VMEM((width, hid), b16),
            pltpu.SemaphoreType.DMA((6 + parts,)),
        ],
        compiler_params=pltpu.CompilerParams(vmem_limit_bytes=24 * MIB),
        cost_estimate=FREE,
    )(
        still_logits,
        stays(tok_feats),
        stays(slot_params.T),
        stays(slot_outputs[0]),
        stays(slot_inputs),
        still_in,
        still_out,
    )

    send = pl.pallas_call(
        functools.partial(expert_kernel, clip_count, seq_count, chunk, wide),
        out_shape=jax.ShapeDtypeStruct((device_count, local_slots, width), b16),
        in_specs=[WHOLE, WHOLE, STAYS, STAYS, STAYS],
        out_specs=WHOLE,
        scratch_shapes=[
            pltpu.VMEM((feed_rows, hid), f32),
            pltpu.VMEM((width, hid), b16),
            pltpu.VMEM((max(hid - kept_rows, chunk), width), b16),
            pltpu.VMEM((feed_rows, kept_rows), f32),
            pltpu.VMEM((feed_rows, hid), b16),
            pltpu.SemaphoreType.DMA(((hid - kept_rows) // chunk + hid // wide + 1,)),
        ],
        compiler_params=pltpu.CompilerParams(vmem_limit_bytes=20 * MIB),
        cost_estimate=pl.CostEstimate(
            flops=4 * feed_rows * width * hid,
            bytes_accessed=4 * width * hid,
            transcendentals=0,
        ),
    )(
        received,
        pltpu.with_memory_space_constraint(kept, pltpu.VMEM),
        stays(slope),
        still_in,
        still_out,
    )
    returned = lax.all_to_all(send, ROUND, split_axis=0, concat_axis=0, tiled=True)

    held = {0: own}
    for bit in seq_bits():
        for other in list(held):
            held[other ^ bit] = swap(held[other] if other == 0 else after(held[other], send), bit)
    dispatch, comb_logit, token_sum, param_all = pl.pallas_call(
        functools.partial(weight_kernel, seq_count),
        out_shape=(
            jax.ShapeDtypeStruct((token_total, slot_total), f32),
            jax.ShapeDtypeStruct((token_total, slot_total), f32),
            jax.ShapeDtypeStruct((slot_total, width), b16),
            jax.ShapeDtypeStruct((slot_total, width), b16),
        ),
        in_specs=[pl.BlockSpec(memory_space=pltpu.SMEM), STAYS, STAYS] + [WHOLE] * seq_count + [PLACED],
        out_specs=(WHOLE,) * 4,
        scratch_shapes=[
            pltpu.VMEM((slot_total, width), b16),
            pltpu.VMEM((token_total, slot_total), b16),
            pltpu.VMEM((token_total, width), b16),
            pltpu.SemaphoreType.DMA((2,)),
        ],
        compiler_params=pltpu.CompilerParams(vmem_limit_bytes=32 * MIB),
        cost_estimate=FREE,
    )(
        lax.axis_index("seq")[None],
        still_logits,
        still_grad,
        *[held[other] for other in range(seq_count)],
        send,
    )

    step = math.gcd(token_total, 128)
    token_grad = pl.pallas_call(
        functools.partial(token_kernel, seq_count, step),
        out_shape=jax.ShapeDtypeStruct((token_total, width), b16),
        in_specs=[WHOLE] * 6,
        out_specs=PLACED,
        scratch_shapes=[
            pltpu.VMEM((token_total, width), b16),
            pltpu.SemaphoreType.DMA((token_total // step,)),
        ],
        compiler_params=pltpu.CompilerParams(vmem_limit_bytes=16 * MIB),
        cost_estimate=pl.CostEstimate(
            flops=6 * token_total * width * slot_total,
            bytes_accessed=4 * token_total * width,
            transcendentals=0,
        ),
    )(
        tok_feats,
        returned,
        token_sum,
        dispatch,
        comb_logit,
        param_all,
    )
    return token_grad[None]


def solution(mesh):
    placed = (
        P("clip", "seq", None),
        P("clip", "seq", None),
        P("clip", "seq", None),
        P(None, "seq"),
        P(None, BOTH, None),
        P("clip", "seq", None),
        P(BOTH, None, None),
        P(BOTH, None, None),
    )
    return jax.shard_map(
        on_device, mesh=mesh, in_specs=placed, out_specs=P("clip", "seq", None), check_vma=False
    )
```

```python
import functools
import math
import random
import jax
import jax.numpy as jnp
from jax import lax
from jax.experimental import pallas as pl
from jax.experimental.pallas import tpu as pltpu
from jax.sharding import PartitionSpec as P

BOTH = ("clip", "seq")
WHOLE = pl.BlockSpec(memory_space=pltpu.VMEM)
PLACED = pl.BlockSpec(memory_space=pl.ANY)
STAYS = pl.BlockSpec(memory_space=pltpu.HBM)
GROUP = 128
SHUFFLE = (1, 25)
MIB = 1 << 20
FREE = pl.CostEstimate(flops=0, bytes_accessed=0, transcendentals=0)


def dot_nn(a, b):
    return jnp.dot(a, b, preferred_element_type=jnp.float32)


def dot_nt(a, b):
    return lax.dot_general(a, b, (((1,), (1,)), ((), ())), preferred_element_type=jnp.float32)


def dot_tn(a, b):
    return lax.dot_general(a, b, (((0,), (0,)), ((), ())), preferred_element_type=jnp.float32)


def exchange_order(devices):
    shuffler = random.Random(SHUFFLE[0])
    for _ in range(SHUFFLE[1]):
        order = list(range(devices))
        shuffler.shuffle(order)
    return order


def exchange(blocks, order):
    return lax.all_to_all(
        blocks, BOTH, split_axis=0, concat_axis=0, axis_index_groups=[order], tiled=True
    )


def fetch(pairs, sems):
    copies = [
        pltpu.make_async_copy(source, held, sems.at[at]) for at, (source, held) in enumerate(pairs)
    ]
    for copy in copies:
        copy.start()
    return copies


def cot_kernel(order, logit_hbm, grad_hbm, out_ref, logit_ref, grad_ref, sems):
    got_logits, got_grad = fetch([(logit_hbm, logit_ref), (grad_hbm, grad_ref)], sems)
    got_logits.wait()
    scores = logit_ref[...].astype(jnp.float32)
    raised = jnp.exp(scores - jnp.max(scores, axis=1, keepdims=True))
    combine = raised / jnp.sum(raised, axis=1, keepdims=True)
    got_grad.wait()
    cot = dot_tn(combine.astype(jnp.bfloat16), grad_ref[...])
    cot = cot.reshape(out_ref.shape)
    for place, device in enumerate(order):
        out_ref[place] = cot[device].astype(jnp.bfloat16)


def expert_kernel(
    order, clips, seqs, chunk, wide, got_ref, kept_ref, slope_hbm, in_hbm, out_hbm, send_ref,
    slope_ref, in_ref, out_ref, act_ref, cot_ref, sems
):
    rows, width = got_ref.shape[1:]
    hid, kept = in_hbm.shape[1], kept_ref.shape[0]
    outs, ins = (hid - kept) // chunk, hid // wide

    def place(part, size, shift=0):
        return pl.ds(pl.multiple_of(shift + part * size, GROUP), size)

    def out_copy(part):
        return pltpu.make_async_copy(
            out_hbm.at[place(part, chunk, kept), :], out_ref.at[place(part, chunk), :], sems.at[part]
        )

    def in_copy(part):
        at = place(part, wide)
        return pltpu.make_async_copy(in_hbm.at[:, at], in_ref.at[:, at], sems.at[outs + part])

    slope_copy = pltpu.make_async_copy(slope_hbm, slope_ref, sems.at[outs + ins])
    slope_copy.start()
    for part in range(outs):
        out_copy(part).start()
    for part in range(ins):
        in_copy(part).start()
    got = [got_ref[order.index(device)].astype(jnp.float32) for device in range(clips * seqs)]
    cot = [sum(got[clip * seqs : (clip + 1) * seqs]) for clip in range(clips)]
    cot = jnp.concatenate(cot, axis=0).astype(jnp.bfloat16)

    @pl.loop(0, kept // chunk)
    def _(part):
        at = place(part, chunk)
        act_ref[:, at] = dot_nt(cot, kept_ref[at, :])

    slope_copy.wait()
    cot_ref[:, :kept] = (act_ref[...] * slope_ref[:, :kept]).astype(jnp.bfloat16)

    @pl.loop(0, outs)
    def _(part):
        out_copy(part).wait()
        at = place(part, chunk, kept)
        act_cot = dot_nt(cot, out_ref[place(part, chunk), :])
        cot_ref[:, at] = (act_cot * slope_ref[:, at]).astype(jnp.bfloat16)

    def add(part, total):
        in_copy(part).wait()
        at = place(part, wide)
        return total + dot_nt(cot_ref[:, at], in_ref[:, at])

    grad = lax.fori_loop(0, ins, add, jnp.zeros((clips * rows, width), jnp.float32))
    grad = grad.reshape(clips, rows, width).astype(jnp.bfloat16)
    for at, device in enumerate(order):
        send_ref[at] = grad[device // seqs]


def token_kernel(
    order, chunk, tok_ref, got_ref, sum_ref, disp_ref, comb_ref, param_ref,
    out_hbm, stage, sems
):
    slots = param_ref.shape[0]
    slot_grad = [got_ref[order.index(at)].astype(jnp.float32) for at in range(len(order))]
    slot_grad = jnp.concatenate(slot_grad, axis=0).astype(jnp.bfloat16)
    cross = dot_nt(sum_ref[...], slot_grad)
    row = lax.broadcasted_iota(jnp.int32, (slots, slots), 0)
    col = lax.broadcasted_iota(jnp.int32, (slots, slots), 1)
    slot_dots = jnp.sum(jnp.where(row == col, cross, 0.0), axis=0, keepdims=True)
    both_rows = jnp.concatenate([slot_grad, param_ref[...]], axis=0)
    copies = []
    for step in range(tok_ref.shape[0] // chunk):
        part = pl.ds(step * chunk, chunk)
        dispatch = disp_ref[part, :]
        disp_cot = dot_nt(tok_ref[part, :], slot_grad)
        logit_grad = comb_ref[part, :] + dispatch * (disp_cot - slot_dots)
        weights = jnp.concatenate([dispatch, logit_grad], axis=1).astype(jnp.bfloat16)
        stage[part, :] = dot_nn(weights, both_rows).astype(jnp.bfloat16)
        copy = pltpu.make_async_copy(stage.at[part, :], out_hbm.at[part, :], sems.at[step])
        copy.start()
        copies.append(copy)
    for copy in copies:
        copy.wait()


def stays(value):
    return pltpu.with_memory_space_constraint(value, pltpu.HBM)


def after(value, token):
    return lax.optimization_barrier((value, token))[0]


def seq_bits():
    count = lax.axis_size("seq")
    return [1 << place for place in reversed(range(count.bit_length() - 1))]


def swap(value, bit):
    count = lax.axis_size("seq")
    return lax.ppermute(value, "seq", [(i, i ^ bit) for i in range(count)])


def stat_places(slots, width):
    groups, per_row = slots // GROUP, width // GROUP
    return [
        [(g * GROUP, (v * groups + g) // per_row, (v * groups + g) % per_row * GROUP) for g in range(groups)]
        for v in range(4)
    ]


def stat_rows(slots, width):
    return -(-4 * slots // (16 * width)) * 16


def side_kernel(
    parts, logit_hbm, tok_hbm, param_hbm, slot_hbm, feed_hbm, in_hbm, out_hbm,
    pack_ref, slope_ref, kept_ref, logit_ref, tok_ref, feed_ref, stat_ref, in_ref, sems
):
    slots, width = logit_ref.shape[1], tok_ref.shape[1]
    seq_slots = slot_hbm.shape[0]
    hid = in_hbm.shape[1]
    places = [pl.ds(part * (hid // parts), hid // parts) for part in range(parts)]
    copies = fetch(
        [
            (logit_hbm, logit_ref),
            (tok_hbm, tok_ref),
            (param_hbm, pack_ref.at[pl.ds(slots, seq_slots)]),
            (slot_hbm, pack_ref.at[pl.ds(slots + seq_slots, seq_slots)]),
            (feed_hbm, feed_ref),
        ]
        + [(in_hbm.at[:, at], in_ref.at[:, at]) for at in places]
        + [(out_hbm.at[pl.ds(0, kept_ref.shape[0])], kept_ref)],
        sems,
    )
    copies[0].wait()
    scores = logit_ref[...].astype(jnp.float32)
    highest = jnp.max(scores, axis=0, keepdims=True)
    raised = jnp.exp(scores - highest)
    total = jnp.sum(raised, axis=0, keepdims=True)
    part0 = total.astype(jnp.bfloat16).astype(jnp.float32)
    part1 = (total - part0).astype(jnp.bfloat16).astype(jnp.float32)
    part2 = total - part0 - part1
    stat_ref[...] = jnp.zeros_like(stat_ref)
    for vector, spots in zip((highest, part0, part1, part2), stat_places(slots, width)):
        for slot, row, lane in spots:
            stat_ref[row : row + 1, lane : lane + GROUP] = vector[:, slot : slot + GROUP]
    pack_ref[slots + 2 * seq_slots :] = stat_ref[...].astype(jnp.bfloat16)
    copies[1].wait()
    pack_ref[:slots] = dot_tn(raised.astype(jnp.bfloat16), tok_ref[...]).astype(jnp.bfloat16)
    copies[4].wait()
    feed = [feed_ref[clip].astype(jnp.float32) for clip in range(feed_ref.shape[0])]
    feed = jnp.concatenate(feed, axis=0).astype(jnp.bfloat16)
    root = math.sqrt(2.0 / math.pi)
    for at, copy in zip(places, copies[5:]):
        copy.wait()
        x = dot_nn(feed, in_ref[:, at])
        bend = jnp.tanh(root * (x + 0.044715 * (x * x * x)))
        grown = root * (1.0 + 3.0 * 0.044715 * (x * x))
        slope_ref[:, at] = 0.5 * (1.0 + bend) + 0.5 * x * (1.0 - bend * bend) * grown
    copies[2].wait()
    copies[3].wait()
    copies[-1].wait()


def weight_kernel(seqs, me_ref, logit_hbm, grad_hbm, *refs):
    packs, (disp_ref, comb_ref, sum_ref, param_ref) = list(refs[:seqs]), refs[seqs + 1 : seqs + 5]
    slot_ref, logit_ref, grad_ref, early_ref, sems = refs[seqs + 5 :]
    slots, width = logit_ref.shape[1], grad_ref.shape[1]
    early = [(packs[other], early_ref.at[other // 2]) for other in range(0, seqs, 2)]
    got_logits, *got_early, got_grad = fetch(
        [(logit_hbm, logit_ref)] + early + [(grad_hbm, grad_ref)], sems
    )
    got_logits.wait()
    scores = logit_ref[...].astype(jnp.float32)
    raised = jnp.exp(scores - jnp.max(scores, axis=1, keepdims=True))
    combine = raised / jnp.sum(raised, axis=1, keepdims=True)
    for other in range(0, seqs, 2):
        got_early[other // 2].wait()
        packs[other] = early_ref.at[other // 2]
    seq_slots = slots // seqs
    me = me_ref[0]
    stats = []
    for other, pack in enumerate(packs):
        base = slots + 2 * seq_slots
        rows = pack[base : base + stat_rows(slots, width)].astype(jnp.float32)
        parts = [
            jnp.concatenate([rows[r : r + 1, lane : lane + GROUP] for _, r, lane in places], axis=1)
            for places in stat_places(slots, width)
        ]
        stats.append((parts[0], parts[1] + parts[2] + parts[3]))
        at = pl.ds(pl.multiple_of((me ^ other) * seq_slots, seq_slots), seq_slots)
        param_ref[at, :] = pack[slots : slots + seq_slots]
        slot_ref[at, :] = pack[slots + seq_slots : slots + 2 * seq_slots]
    highest = functools.reduce(jnp.maximum, [top for top, _ in stats])
    total = sum(part * jnp.exp(top - highest) for top, part in stats)
    row = lax.broadcasted_iota(jnp.int32, (slots, slots), 0)
    col = lax.broadcasted_iota(jnp.int32, (slots, slots), 1)
    token_sum = jnp.zeros((slots, width), jnp.float32)
    for pack, (top, _) in zip(packs, stats):
        share = jnp.exp(top - highest) / total
        share = jnp.sum(jnp.where(row == col, share, 0.0), axis=1, keepdims=True)
        token_sum += share * pack[:slots].astype(jnp.float32)
    sum_ref[...] = token_sum.astype(jnp.bfloat16)
    disp_ref[...] = jnp.exp(scores - highest) / total
    got_grad.wait()
    comb_cot = dot_nt(grad_ref[...], slot_ref[...])
    comb_ref[...] = combine * (comb_cot - jnp.sum(combine * comb_cot, axis=1, keepdims=True))


def on_device(
    tokens, out_grad, saved_logits, slot_params, slot_inputs, slot_outputs, expert_in, expert_out
):
    clip_count = lax.axis_size("clip")
    seq_count = lax.axis_size("seq")
    device_count = clip_count * seq_count
    order = exchange_order(device_count)
    tok_feats, out_cot, logit_raw = tokens[0], out_grad[0], saved_logits[0]
    token_total, width = tok_feats.shape
    slot_total = logit_raw.shape[1]
    clip_total, local_slots = slot_inputs.shape[:2]
    hid = expert_in.shape[2]
    feed_rows = clip_total * local_slots
    f32, b16 = jnp.float32, jnp.bfloat16

    still_logits, still_grad = stays(logit_raw), stays(out_cot)
    still_in, still_out = stays(expert_in[0]), stays(expert_out[0])
    blocks = pl.pallas_call(
        functools.partial(cot_kernel, order),
        out_shape=jax.ShapeDtypeStruct((device_count, local_slots, width), b16),
        in_specs=[STAYS, STAYS],
        out_specs=WHOLE,
        scratch_shapes=[
            pltpu.VMEM((token_total, slot_total), b16),
            pltpu.VMEM((token_total, width), b16),
            pltpu.SemaphoreType.DMA((2,)),
        ],
        compiler_params=pltpu.CompilerParams(vmem_limit_bytes=16 * MIB),
        cost_estimate=FREE,
    )(still_logits, still_grad)
    received = exchange(blocks, order)

    parts = math.gcd(hid // GROUP, 4)
    seq_slots = slot_params.shape[1]
    pack_rows = slot_total + 2 * seq_slots + stat_rows(slot_total, width)
    pieces = math.gcd(hid // GROUP, 6)
    chunk, wide = hid // pieces, hid // math.gcd(pieces, 3)
    kept_rows = max(pieces // 2, 1) * chunk
    own, slope, kept = pl.pallas_call(
        functools.partial(side_kernel, parts),
        out_shape=(
            jax.ShapeDtypeStruct((pack_rows, width), b16),
            pltpu.HBM((feed_rows, hid), f32),
            pltpu.VMEM((kept_rows, width), b16),
        ),
        in_specs=[STAYS] * 7,
        out_specs=(WHOLE,) * 3,
        scratch_shapes=[
            pltpu.VMEM((token_total, slot_total), b16),
            pltpu.VMEM((token_total, width), b16),
            pltpu.VMEM(slot_inputs.shape, b16),
            pltpu.VMEM((stat_rows(slot_total, width), width), f32),
            pltpu.VMEM((width, hid), b16),
            pltpu.SemaphoreType.DMA((6 + parts,)),
        ],
        compiler_params=pltpu.CompilerParams(vmem_limit_bytes=24 * MIB),
        cost_estimate=FREE,
    )(
        still_logits,
        stays(tok_feats),
        stays(slot_params.T),
        stays(slot_outputs[0]),
        stays(slot_inputs),
        still_in,
        still_out,
    )

    send = pl.pallas_call(
        functools.partial(expert_kernel, order, clip_count, seq_count, chunk, wide),
        out_shape=jax.ShapeDtypeStruct((device_count, local_slots, width), b16),
        in_specs=[WHOLE, WHOLE, STAYS, STAYS, STAYS],
        out_specs=WHOLE,
        scratch_shapes=[
            pltpu.VMEM((feed_rows, hid), f32),
            pltpu.VMEM((width, hid), b16),
            pltpu.VMEM((max(hid - kept_rows, chunk), width), b16),
            pltpu.VMEM((feed_rows, kept_rows), f32),
            pltpu.VMEM((feed_rows, hid), b16),
            pltpu.SemaphoreType.DMA(((hid - kept_rows) // chunk + hid // wide + 1,)),
        ],
        compiler_params=pltpu.CompilerParams(vmem_limit_bytes=20 * MIB),
        cost_estimate=pl.CostEstimate(
            flops=4 * feed_rows * width * hid,
            bytes_accessed=4 * width * hid,
            transcendentals=0,
        ),
    )(
        received,
        pltpu.with_memory_space_constraint(kept, pltpu.VMEM),
        stays(slope),
        still_in,
        still_out,
    )
    returned = exchange(send, order)

    held = {0: own}
    for bit in seq_bits():
        for other in list(held):
            held[other ^ bit] = swap(held[other] if other == 0 else after(held[other], send), bit)
    dispatch, comb_logit, token_sum, param_all = pl.pallas_call(
        functools.partial(weight_kernel, seq_count),
        out_shape=(
            jax.ShapeDtypeStruct((token_total, slot_total), f32),
            jax.ShapeDtypeStruct((token_total, slot_total), f32),
            jax.ShapeDtypeStruct((slot_total, width), b16),
            jax.ShapeDtypeStruct((slot_total, width), b16),
        ),
        in_specs=[pl.BlockSpec(memory_space=pltpu.SMEM), STAYS, STAYS]
        + [STAYS if other % 2 == 0 else WHOLE for other in range(seq_count)]
        + [PLACED],
        out_specs=(WHOLE,) * 4,
        scratch_shapes=[
            pltpu.VMEM((slot_total, width), b16),
            pltpu.VMEM((token_total, slot_total), b16),
            pltpu.VMEM((token_total, width), b16),
            pltpu.VMEM(((seq_count + 1) // 2, pack_rows, width), b16),
            pltpu.SemaphoreType.DMA((2 + (seq_count + 1) // 2,)),
        ],
        compiler_params=pltpu.CompilerParams(vmem_limit_bytes=48 * MIB),
        cost_estimate=FREE,
    )(
        lax.axis_index("seq")[None],
        still_logits,
        still_grad,
        *[stays(held[at]) if at % 2 == 0 else held[at] for at in range(seq_count)],
        send,
    )

    step = math.gcd(token_total, 128)
    token_grad = pl.pallas_call(
        functools.partial(token_kernel, order, step),
        out_shape=jax.ShapeDtypeStruct((token_total, width), b16),
        in_specs=[WHOLE] * 6,
        out_specs=PLACED,
        scratch_shapes=[
            pltpu.VMEM((token_total, width), b16),
            pltpu.SemaphoreType.DMA((token_total // step,)),
        ],
        compiler_params=pltpu.CompilerParams(vmem_limit_bytes=16 * MIB),
        cost_estimate=pl.CostEstimate(
            flops=6 * token_total * width * slot_total,
            bytes_accessed=4 * token_total * width,
            transcendentals=0,
        ),
    )(
        tok_feats,
        returned,
        token_sum,
        dispatch,
        comb_logit,
        param_all,
    )
    return token_grad[None]


def solution(mesh):
    placed = (
        P("clip", "seq", None),
        P("clip", "seq", None),
        P("clip", "seq", None),
        P(None, "seq"),
        P(None, BOTH, None),
        P("clip", "seq", None),
        P(BOTH, None, None),
        P(BOTH, None, None),
    )
    return jax.shard_map(
        on_device, mesh=mesh, in_specs=placed, out_specs=P("clip", "seq", None), check_vma=False
    )
```

```python
import functools
import math
import random
import jax
import jax.numpy as jnp
from jax import lax
from jax.experimental import pallas as pl
from jax.experimental.pallas import tpu as pltpu
from jax.sharding import PartitionSpec as P

BOTH = ("clip", "seq")
WHOLE = pl.BlockSpec(memory_space=pltpu.VMEM)
PLACED = pl.BlockSpec(memory_space=pl.ANY)
STAYS = pl.BlockSpec(memory_space=pltpu.HBM)
GROUP = 128
SHUFFLES = ((1, 25), (1, 12))
MIB = 1 << 20
FREE = pl.CostEstimate(flops=0, bytes_accessed=0, transcendentals=0)


def dot_nn(a, b):
    return jnp.dot(a, b, preferred_element_type=jnp.float32)


def dot_nt(a, b):
    return lax.dot_general(a, b, (((1,), (1,)), ((), ())), preferred_element_type=jnp.float32)


def dot_tn(a, b):
    return lax.dot_general(a, b, (((0,), (0,)), ((), ())), preferred_element_type=jnp.float32)


def exchange_order(devices, seed, turns):
    shuffler = random.Random(seed)
    for _ in range(turns):
        order = list(range(devices))
        shuffler.shuffle(order)
    return order


def exchange(blocks, order):
    return lax.all_to_all(
        blocks, BOTH, split_axis=0, concat_axis=0, axis_index_groups=[order], tiled=True
    )


def fetch(pairs, sems):
    copies = [
        pltpu.make_async_copy(source, held, sems.at[at]) for at, (source, held) in enumerate(pairs)
    ]
    for copy in copies:
        copy.start()
    return copies


def cot_kernel(order, logit_hbm, grad_hbm, out_ref, logit_ref, grad_ref, sems):
    got_logits, got_grad = fetch([(logit_hbm, logit_ref), (grad_hbm, grad_ref)], sems)
    got_logits.wait()
    scores = logit_ref[...].astype(jnp.float32)
    raised = jnp.exp(scores - jnp.max(scores, axis=1, keepdims=True))
    combine = raised / jnp.sum(raised, axis=1, keepdims=True)
    got_grad.wait()
    cot = dot_tn(combine.astype(jnp.bfloat16), grad_ref[...])
    cot = cot.reshape(out_ref.shape)
    for place, device in enumerate(order):
        out_ref[place] = cot[device].astype(jnp.bfloat16)


def expert_kernel(
    there, back, clips, seqs, chunk, wide, got_ref, kept_ref, slope_hbm, in_hbm, out_hbm, send_ref,
    slope_ref, in_ref, out_ref, act_ref, cot_ref, sems
):
    rows, width = got_ref.shape[1:]
    hid, kept = in_hbm.shape[1], kept_ref.shape[0]
    outs, ins = (hid - kept) // chunk, hid // wide

    def place(part, size, shift=0):
        return pl.ds(pl.multiple_of(shift + part * size, GROUP), size)

    def out_copy(part):
        return pltpu.make_async_copy(
            out_hbm.at[place(part, chunk, kept), :], out_ref.at[place(part, chunk), :], sems.at[part]
        )

    def in_copy(part):
        at = place(part, wide)
        return pltpu.make_async_copy(in_hbm.at[:, at], in_ref.at[:, at], sems.at[outs + part])

    slope_copy = pltpu.make_async_copy(slope_hbm, slope_ref, sems.at[outs + ins])
    slope_copy.start()
    for part in range(outs):
        out_copy(part).start()
    for part in range(ins):
        in_copy(part).start()
    got = [got_ref[there.index(device)].astype(jnp.float32) for device in range(clips * seqs)]
    cot = [sum(got[clip * seqs : (clip + 1) * seqs]) for clip in range(clips)]
    cot = jnp.concatenate(cot, axis=0).astype(jnp.bfloat16)

    @pl.loop(0, kept // chunk)
    def _(part):
        at = place(part, chunk)
        act_ref[:, at] = dot_nt(cot, kept_ref[at, :])

    slope_copy.wait()
    cot_ref[:, :kept] = (act_ref[...] * slope_ref[:, :kept]).astype(jnp.bfloat16)

    @pl.loop(0, outs)
    def _(part):
        out_copy(part).wait()
        at = place(part, chunk, kept)
        act_cot = dot_nt(cot, out_ref[place(part, chunk), :])
        cot_ref[:, at] = (act_cot * slope_ref[:, at]).astype(jnp.bfloat16)

    def add(part, total):
        in_copy(part).wait()
        at = place(part, wide)
        return total + dot_nt(cot_ref[:, at], in_ref[:, at])

    grad = lax.fori_loop(0, ins, add, jnp.zeros((clips * rows, width), jnp.float32))
    grad = grad.reshape(clips, rows, width).astype(jnp.bfloat16)
    for at, device in enumerate(back):
        send_ref[at] = grad[device // seqs]


def token_kernel(
    order, chunk, tok_ref, got_ref, sum_ref, disp_ref, comb_ref, param_ref,
    out_hbm, stage, sems
):
    slots = param_ref.shape[0]
    slot_grad = [got_ref[order.index(at)].astype(jnp.float32) for at in range(len(order))]
    slot_grad = jnp.concatenate(slot_grad, axis=0).astype(jnp.bfloat16)
    cross = dot_nt(sum_ref[...], slot_grad)
    row = lax.broadcasted_iota(jnp.int32, (slots, slots), 0)
    col = lax.broadcasted_iota(jnp.int32, (slots, slots), 1)
    slot_dots = jnp.sum(jnp.where(row == col, cross, 0.0), axis=0, keepdims=True)
    both_rows = jnp.concatenate([slot_grad, param_ref[...]], axis=0)
    copies = []
    for step in range(tok_ref.shape[0] // chunk):
        part = pl.ds(step * chunk, chunk)
        dispatch = disp_ref[part, :]
        disp_cot = dot_nt(tok_ref[part, :], slot_grad)
        logit_grad = comb_ref[part, :] + dispatch * (disp_cot - slot_dots)
        weights = jnp.concatenate([dispatch, logit_grad], axis=1).astype(jnp.bfloat16)
        stage[part, :] = dot_nn(weights, both_rows).astype(jnp.bfloat16)
        copy = pltpu.make_async_copy(stage.at[part, :], out_hbm.at[part, :], sems.at[step])
        copy.start()
        copies.append(copy)
    for copy in copies:
        copy.wait()


def stays(value):
    return pltpu.with_memory_space_constraint(value, pltpu.HBM)


def after(value, token):
    return lax.optimization_barrier((value, token))[0]


def seq_bits():
    count = lax.axis_size("seq")
    return [1 << place for place in reversed(range(count.bit_length() - 1))]


def swap(value, bit):
    count = lax.axis_size("seq")
    return lax.ppermute(value, "seq", [(i, i ^ bit) for i in range(count)])


def stat_places(slots, width):
    groups, per_row = slots // GROUP, width // GROUP
    return [
        [(g * GROUP, (v * groups + g) // per_row, (v * groups + g) % per_row * GROUP) for g in range(groups)]
        for v in range(4)
    ]


def stat_rows(slots, width):
    return -(-4 * slots // (16 * width)) * 16


def side_kernel(
    parts, logit_hbm, tok_hbm, param_hbm, slot_hbm, feed_hbm, in_hbm, out_hbm,
    pack_ref, slope_ref, kept_ref, logit_ref, tok_ref, feed_ref, stat_ref, in_ref, sems
):
    slots, width = logit_ref.shape[1], tok_ref.shape[1]
    seq_slots = slot_hbm.shape[0]
    hid = in_hbm.shape[1]
    places = [pl.ds(part * (hid // parts), hid // parts) for part in range(parts)]
    copies = fetch(
        [
            (logit_hbm, logit_ref),
            (tok_hbm, tok_ref),
            (param_hbm, pack_ref.at[pl.ds(slots, seq_slots)]),
            (slot_hbm, pack_ref.at[pl.ds(slots + seq_slots, seq_slots)]),
            (feed_hbm, feed_ref),
        ]
        + [(in_hbm.at[:, at], in_ref.at[:, at]) for at in places]
        + [(out_hbm.at[pl.ds(0, kept_ref.shape[0])], kept_ref)],
        sems,
    )
    copies[0].wait()
    scores = logit_ref[...].astype(jnp.float32)
    highest = jnp.max(scores, axis=0, keepdims=True)
    raised = jnp.exp(scores - highest)
    total = jnp.sum(raised, axis=0, keepdims=True)
    part0 = total.astype(jnp.bfloat16).astype(jnp.float32)
    part1 = (total - part0).astype(jnp.bfloat16).astype(jnp.float32)
    part2 = total - part0 - part1
    stat_ref[...] = jnp.zeros_like(stat_ref)
    for vector, spots in zip((highest, part0, part1, part2), stat_places(slots, width)):
        for slot, row, lane in spots:
            stat_ref[row : row + 1, lane : lane + GROUP] = vector[:, slot : slot + GROUP]
    pack_ref[slots + 2 * seq_slots :] = stat_ref[...].astype(jnp.bfloat16)
    copies[1].wait()
    pack_ref[:slots] = dot_tn(raised.astype(jnp.bfloat16), tok_ref[...]).astype(jnp.bfloat16)
    copies[4].wait()
    feed = [feed_ref[clip].astype(jnp.float32) for clip in range(feed_ref.shape[0])]
    feed = jnp.concatenate(feed, axis=0).astype(jnp.bfloat16)
    root = math.sqrt(2.0 / math.pi)
    for at, copy in zip(places, copies[5:]):
        copy.wait()
        x = dot_nn(feed, in_ref[:, at])
        bend = jnp.tanh(root * (x + 0.044715 * (x * x * x)))
        grown = root * (1.0 + 3.0 * 0.044715 * (x * x))
        slope_ref[:, at] = 0.5 * (1.0 + bend) + 0.5 * x * (1.0 - bend * bend) * grown
    copies[2].wait()
    copies[3].wait()
    copies[-1].wait()


def weight_kernel(seqs, me_ref, logit_hbm, grad_hbm, *refs):
    packs, (disp_ref, comb_ref, sum_ref, param_ref) = list(refs[:seqs]), refs[seqs + 1 : seqs + 5]
    slot_ref, logit_ref, grad_ref, early_ref, sems = refs[seqs + 5 :]
    slots, width = logit_ref.shape[1], grad_ref.shape[1]
    early = [(packs[other], early_ref.at[other // 2]) for other in range(0, seqs, 2)]
    got_logits, *got_early, got_grad = fetch(
        [(logit_hbm, logit_ref)] + early + [(grad_hbm, grad_ref)], sems
    )
    got_logits.wait()
    scores = logit_ref[...].astype(jnp.float32)
    raised = jnp.exp(scores - jnp.max(scores, axis=1, keepdims=True))
    combine = raised / jnp.sum(raised, axis=1, keepdims=True)
    for other in range(0, seqs, 2):
        got_early[other // 2].wait()
        packs[other] = early_ref.at[other // 2]
    seq_slots = slots // seqs
    me = me_ref[0]
    stats = []
    for other, pack in enumerate(packs):
        base = slots + 2 * seq_slots
        rows = pack[base : base + stat_rows(slots, width)].astype(jnp.float32)
        parts = [
            jnp.concatenate([rows[r : r + 1, lane : lane + GROUP] for _, r, lane in places], axis=1)
            for places in stat_places(slots, width)
        ]
        stats.append((parts[0], parts[1] + parts[2] + parts[3]))
        at = pl.ds(pl.multiple_of((me ^ other) * seq_slots, seq_slots), seq_slots)
        param_ref[at, :] = pack[slots : slots + seq_slots]
        slot_ref[at, :] = pack[slots + seq_slots : slots + 2 * seq_slots]
    highest = functools.reduce(jnp.maximum, [top for top, _ in stats])
    total = sum(part * jnp.exp(top - highest) for top, part in stats)
    row = lax.broadcasted_iota(jnp.int32, (slots, slots), 0)
    col = lax.broadcasted_iota(jnp.int32, (slots, slots), 1)
    token_sum = jnp.zeros((slots, width), jnp.float32)
    for pack, (top, _) in zip(packs, stats):
        share = jnp.exp(top - highest) / total
        share = jnp.sum(jnp.where(row == col, share, 0.0), axis=1, keepdims=True)
        token_sum += share * pack[:slots].astype(jnp.float32)
    sum_ref[...] = token_sum.astype(jnp.bfloat16)
    disp_ref[...] = jnp.exp(scores - highest) / total
    got_grad.wait()
    comb_cot = dot_nt(grad_ref[...], slot_ref[...])
    comb_ref[...] = combine * (comb_cot - jnp.sum(combine * comb_cot, axis=1, keepdims=True))


def on_device(
    tokens, out_grad, saved_logits, slot_params, slot_inputs, slot_outputs, expert_in, expert_out
):
    clip_count = lax.axis_size("clip")
    seq_count = lax.axis_size("seq")
    device_count = clip_count * seq_count
    there, back = (exchange_order(device_count, *seed) for seed in SHUFFLES)
    tok_feats, out_cot, logit_raw = tokens[0], out_grad[0], saved_logits[0]
    token_total, width = tok_feats.shape
    slot_total = logit_raw.shape[1]
    clip_total, local_slots = slot_inputs.shape[:2]
    hid = expert_in.shape[2]
    feed_rows = clip_total * local_slots
    f32, b16 = jnp.float32, jnp.bfloat16

    still_logits, still_grad = stays(logit_raw), stays(out_cot)
    still_in, still_out = stays(expert_in[0]), stays(expert_out[0])
    blocks = pl.pallas_call(
        functools.partial(cot_kernel, there),
        out_shape=jax.ShapeDtypeStruct((device_count, local_slots, width), b16),
        in_specs=[STAYS, STAYS],
        out_specs=WHOLE,
        scratch_shapes=[
            pltpu.VMEM((token_total, slot_total), b16),
            pltpu.VMEM((token_total, width), b16),
            pltpu.SemaphoreType.DMA((2,)),
        ],
        compiler_params=pltpu.CompilerParams(vmem_limit_bytes=16 * MIB),
        cost_estimate=FREE,
    )(still_logits, still_grad)
    received = exchange(blocks, there)

    parts = math.gcd(hid // GROUP, 4)
    seq_slots = slot_params.shape[1]
    pack_rows = slot_total + 2 * seq_slots + stat_rows(slot_total, width)
    pieces = math.gcd(hid // GROUP, 6)
    chunk, wide = hid // pieces, hid // math.gcd(pieces, 3)
    kept_rows = max(pieces // 2, 1) * chunk
    own, slope, kept = pl.pallas_call(
        functools.partial(side_kernel, parts),
        out_shape=(
            jax.ShapeDtypeStruct((pack_rows, width), b16),
            pltpu.HBM((feed_rows, hid), f32),
            pltpu.VMEM((kept_rows, width), b16),
        ),
        in_specs=[STAYS] * 7,
        out_specs=(WHOLE,) * 3,
        scratch_shapes=[
            pltpu.VMEM((token_total, slot_total), b16),
            pltpu.VMEM((token_total, width), b16),
            pltpu.VMEM(slot_inputs.shape, b16),
            pltpu.VMEM((stat_rows(slot_total, width), width), f32),
            pltpu.VMEM((width, hid), b16),
            pltpu.SemaphoreType.DMA((6 + parts,)),
        ],
        compiler_params=pltpu.CompilerParams(vmem_limit_bytes=24 * MIB),
        cost_estimate=FREE,
    )(
        still_logits,
        stays(tok_feats),
        stays(slot_params.T),
        stays(slot_outputs[0]),
        stays(slot_inputs),
        still_in,
        still_out,
    )

    send = pl.pallas_call(
        functools.partial(expert_kernel, there, back, clip_count, seq_count, chunk, wide),
        out_shape=jax.ShapeDtypeStruct((device_count, local_slots, width), b16),
        in_specs=[WHOLE, WHOLE, STAYS, STAYS, STAYS],
        out_specs=WHOLE,
        scratch_shapes=[
            pltpu.VMEM((feed_rows, hid), f32),
            pltpu.VMEM((width, hid), b16),
            pltpu.VMEM((max(hid - kept_rows, chunk), width), b16),
            pltpu.VMEM((feed_rows, kept_rows), f32),
            pltpu.VMEM((feed_rows, hid), b16),
            pltpu.SemaphoreType.DMA(((hid - kept_rows) // chunk + hid // wide + 1,)),
        ],
        compiler_params=pltpu.CompilerParams(vmem_limit_bytes=20 * MIB),
        cost_estimate=pl.CostEstimate(
            flops=4 * feed_rows * width * hid,
            bytes_accessed=4 * width * hid,
            transcendentals=0,
        ),
    )(
        received,
        pltpu.with_memory_space_constraint(kept, pltpu.VMEM),
        stays(slope),
        still_in,
        still_out,
    )
    returned = exchange(send, back)

    held = {0: own}
    for bit in seq_bits():
        for other in list(held):
            held[other ^ bit] = swap(held[other] if other == 0 else after(held[other], send), bit)
    dispatch, comb_logit, token_sum, param_all = pl.pallas_call(
        functools.partial(weight_kernel, seq_count),
        out_shape=(
            jax.ShapeDtypeStruct((token_total, slot_total), f32),
            jax.ShapeDtypeStruct((token_total, slot_total), f32),
            jax.ShapeDtypeStruct((slot_total, width), b16),
            jax.ShapeDtypeStruct((slot_total, width), b16),
        ),
        in_specs=[pl.BlockSpec(memory_space=pltpu.SMEM), STAYS, STAYS]
        + [STAYS if other % 2 == 0 else WHOLE for other in range(seq_count)]
        + [PLACED],
        out_specs=(WHOLE,) * 4,
        scratch_shapes=[
            pltpu.VMEM((slot_total, width), b16),
            pltpu.VMEM((token_total, slot_total), b16),
            pltpu.VMEM((token_total, width), b16),
            pltpu.VMEM(((seq_count + 1) // 2, pack_rows, width), b16),
            pltpu.SemaphoreType.DMA((2 + (seq_count + 1) // 2,)),
        ],
        compiler_params=pltpu.CompilerParams(vmem_limit_bytes=48 * MIB),
        cost_estimate=FREE,
    )(
        lax.axis_index("seq")[None],
        still_logits,
        still_grad,
        *[stays(held[at]) if at % 2 == 0 else held[at] for at in range(seq_count)],
        send,
    )

    step = math.gcd(token_total, 128)
    token_grad = pl.pallas_call(
        functools.partial(token_kernel, back, step),
        out_shape=jax.ShapeDtypeStruct((token_total, width), b16),
        in_specs=[WHOLE] * 6,
        out_specs=PLACED,
        scratch_shapes=[
            pltpu.VMEM((token_total, width), b16),
            pltpu.SemaphoreType.DMA((token_total // step,)),
        ],
        compiler_params=pltpu.CompilerParams(vmem_limit_bytes=16 * MIB),
        cost_estimate=pl.CostEstimate(
            flops=6 * token_total * width * slot_total,
            bytes_accessed=4 * token_total * width,
            transcendentals=0,
        ),
    )(
        tok_feats,
        returned,
        token_sum,
        dispatch,
        comb_logit,
        param_all,
    )
    return token_grad[None]


def solution(mesh):
    placed = (
        P("clip", "seq", None),
        P("clip", "seq", None),
        P("clip", "seq", None),
        P(None, "seq"),
        P(None, BOTH, None),
        P("clip", "seq", None),
        P(BOTH, None, None),
        P(BOTH, None, None),
    )
    return jax.shard_map(
        on_device, mesh=mesh, in_specs=placed, out_specs=P("clip", "seq", None), check_vma=False
    )
```

```python
import functools
import math
import random
import jax
import jax.numpy as jnp
from jax import lax
from jax.experimental import pallas as pl
from jax.experimental.pallas import tpu as pltpu
from jax.sharding import PartitionSpec as P

BOTH = ("clip", "seq")
WHOLE = pl.BlockSpec(memory_space=pltpu.VMEM)
PLACED = pl.BlockSpec(memory_space=pl.ANY)
STAYS = pl.BlockSpec(memory_space=pltpu.HBM)
GROUP = 128
SHUFFLES = ((1, 25), (1, 12))
MIB = 1 << 20
FREE = pl.CostEstimate(flops=0, bytes_accessed=0, transcendentals=0)


def dot_nn(a, b):
    return jnp.dot(a, b, preferred_element_type=jnp.float32)


def dot_nt(a, b):
    return lax.dot_general(a, b, (((1,), (1,)), ((), ())), preferred_element_type=jnp.float32)


def dot_tn(a, b):
    return lax.dot_general(a, b, (((0,), (0,)), ((), ())), preferred_element_type=jnp.float32)


def exchange_order(devices, seed, turns):
    shuffler = random.Random(seed)
    for _ in range(turns):
        order = list(range(devices))
        shuffler.shuffle(order)
    return order


def exchange(blocks, order):
    return lax.all_to_all(
        blocks, BOTH, split_axis=0, concat_axis=0, axis_index_groups=[order], tiled=True
    )


def fetch(pairs, sems):
    copies = [
        pltpu.make_async_copy(source, held, sems.at[at]) for at, (source, held) in enumerate(pairs)
    ]
    for copy in copies:
        copy.start()
    return copies


def cot_kernel(order, logit_hbm, grad_hbm, out_ref, logit_ref, grad_ref, sems):
    got_logits, got_grad = fetch([(logit_hbm, logit_ref), (grad_hbm, grad_ref)], sems)
    got_logits.wait()
    scores = logit_ref[...].astype(jnp.float32)
    raised = jnp.exp(scores - jnp.max(scores, axis=1, keepdims=True))
    combine = raised / jnp.sum(raised, axis=1, keepdims=True)
    got_grad.wait()
    cot = dot_tn(combine.astype(jnp.bfloat16), grad_ref[...])
    cot = cot.reshape(out_ref.shape)
    for place, device in enumerate(order):
        out_ref[place] = cot[device].astype(jnp.bfloat16)


def expert_kernel(
    there, back, clips, seqs, chunk, wide, got_ref, kept_ref, slope_ref, in_hbm, out_hbm, send_ref,
    in_ref, out_ref, cot_ref, sems
):
    rows, width = got_ref.shape[1:]
    hid, kept = in_hbm.shape[1], kept_ref.shape[0]
    outs, ins = (hid - kept) // chunk, hid // wide

    def place(part, size, shift=0):
        return pl.ds(pl.multiple_of(shift + part * size, GROUP), size)

    def out_copy(part):
        return pltpu.make_async_copy(
            out_hbm.at[place(part, chunk, kept), :], out_ref.at[place(part, chunk), :], sems.at[part]
        )

    def in_copy(part):
        at = place(part, wide)
        return pltpu.make_async_copy(in_hbm.at[:, at], in_ref.at[:, at], sems.at[outs + part])

    for part in range(outs):
        out_copy(part).start()
    for part in range(ins):
        in_copy(part).start()
    got = [got_ref[there.index(device)].astype(jnp.float32) for device in range(clips * seqs)]
    cot = [sum(got[clip * seqs : (clip + 1) * seqs]) for clip in range(clips)]
    cot = jnp.concatenate(cot, axis=0).astype(jnp.bfloat16)

    @pl.loop(0, kept // chunk)
    def _(part):
        at = place(part, chunk)
        cot_ref[:, at] = (dot_nt(cot, kept_ref[at, :]) * slope_ref[:, at]).astype(jnp.bfloat16)

    @pl.loop(0, outs)
    def _(part):
        out_copy(part).wait()
        at = place(part, chunk, kept)
        act_cot = dot_nt(cot, out_ref[place(part, chunk), :])
        cot_ref[:, at] = (act_cot * slope_ref[:, at]).astype(jnp.bfloat16)

    def add(part, total):
        in_copy(part).wait()
        at = place(part, wide)
        return total + dot_nt(cot_ref[:, at], in_ref[:, at])

    grad = lax.fori_loop(0, ins, add, jnp.zeros((clips * rows, width), jnp.float32))
    grad = grad.reshape(clips, rows, width).astype(jnp.bfloat16)
    for at, device in enumerate(back):
        send_ref[at] = grad[device // seqs]


def token_kernel(
    order, chunk, tok_ref, got_ref, sum_ref, disp_ref, comb_ref, param_ref,
    out_hbm, stage, sems
):
    slots = param_ref.shape[0]
    slot_grad = [got_ref[order.index(at)].astype(jnp.float32) for at in range(len(order))]
    slot_grad = jnp.concatenate(slot_grad, axis=0).astype(jnp.bfloat16)
    cross = dot_nt(sum_ref[...], slot_grad)
    row = lax.broadcasted_iota(jnp.int32, (slots, slots), 0)
    col = lax.broadcasted_iota(jnp.int32, (slots, slots), 1)
    slot_dots = jnp.sum(jnp.where(row == col, cross, 0.0), axis=0, keepdims=True)
    both_rows = jnp.concatenate([slot_grad, param_ref[...]], axis=0)
    copies = []
    for step in range(tok_ref.shape[0] // chunk):
        part = pl.ds(step * chunk, chunk)
        dispatch = disp_ref[part, :]
        disp_cot = dot_nt(tok_ref[part, :], slot_grad)
        logit_grad = comb_ref[part, :] + dispatch * (disp_cot - slot_dots)
        weights = jnp.concatenate([dispatch, logit_grad], axis=1).astype(jnp.bfloat16)
        stage[part, :] = dot_nn(weights, both_rows).astype(jnp.bfloat16)
        copy = pltpu.make_async_copy(stage.at[part, :], out_hbm.at[part, :], sems.at[step])
        copy.start()
        copies.append(copy)
    for copy in copies:
        copy.wait()


def stays(value):
    return pltpu.with_memory_space_constraint(value, pltpu.HBM)


def after(value, token):
    return lax.optimization_barrier((value, token))[0]


def seq_bits():
    count = lax.axis_size("seq")
    return [1 << place for place in reversed(range(count.bit_length() - 1))]


def swap(value, bit):
    count = lax.axis_size("seq")
    return lax.ppermute(value, "seq", [(i, i ^ bit) for i in range(count)])


def stat_places(slots, width):
    groups, per_row = slots // GROUP, width // GROUP
    return [
        [(g * GROUP, (v * groups + g) // per_row, (v * groups + g) % per_row * GROUP) for g in range(groups)]
        for v in range(4)
    ]


def stat_rows(slots, width):
    return -(-4 * slots // (16 * width)) * 16


def side_kernel(
    parts, logit_hbm, tok_hbm, param_hbm, slot_hbm, feed_hbm, in_hbm, out_hbm,
    pack_ref, slope_ref, kept_ref, logit_ref, tok_ref, feed_ref, stat_ref, in_ref, sems
):
    slots, width = logit_ref.shape[1], tok_ref.shape[1]
    seq_slots = slot_hbm.shape[0]
    hid = in_hbm.shape[1]
    places = [pl.ds(part * (hid // parts), hid // parts) for part in range(parts)]
    copies = fetch(
        [
            (logit_hbm, logit_ref),
            (tok_hbm, tok_ref),
            (param_hbm, pack_ref.at[pl.ds(slots, seq_slots)]),
            (slot_hbm, pack_ref.at[pl.ds(slots + seq_slots, seq_slots)]),
            (feed_hbm, feed_ref),
        ]
        + [(in_hbm.at[:, at], in_ref.at[:, at]) for at in places]
        + [(out_hbm.at[pl.ds(0, kept_ref.shape[0])], kept_ref)],
        sems,
    )
    copies[0].wait()
    scores = logit_ref[...].astype(jnp.float32)
    highest = jnp.max(scores, axis=0, keepdims=True)
    raised = jnp.exp(scores - highest)
    total = jnp.sum(raised, axis=0, keepdims=True)
    part0 = total.astype(jnp.bfloat16).astype(jnp.float32)
    part1 = (total - part0).astype(jnp.bfloat16).astype(jnp.float32)
    part2 = total - part0 - part1
    stat_ref[...] = jnp.zeros_like(stat_ref)
    for vector, spots in zip((highest, part0, part1, part2), stat_places(slots, width)):
        for slot, row, lane in spots:
            stat_ref[row : row + 1, lane : lane + GROUP] = vector[:, slot : slot + GROUP]
    pack_ref[slots + 2 * seq_slots :] = stat_ref[...].astype(jnp.bfloat16)
    copies[1].wait()
    pack_ref[:slots] = dot_tn(raised.astype(jnp.bfloat16), tok_ref[...]).astype(jnp.bfloat16)
    copies[4].wait()
    feed = [feed_ref[clip].astype(jnp.float32) for clip in range(feed_ref.shape[0])]
    feed = jnp.concatenate(feed, axis=0).astype(jnp.bfloat16)
    root = math.sqrt(2.0 / math.pi)
    for at, copy in zip(places, copies[5:]):
        copy.wait()
        x = dot_nn(feed, in_ref[:, at])
        bend = jnp.tanh(root * (x + 0.044715 * (x * x * x)))
        grown = root * (1.0 + 3.0 * 0.044715 * (x * x))
        slope = 0.5 * (1.0 + bend) + 0.5 * x * (1.0 - bend * bend) * grown
        slope_ref[:, at] = slope.astype(slope_ref.dtype)
    copies[2].wait()
    copies[3].wait()
    copies[-1].wait()


def weight_kernel(seqs, me_ref, logit_hbm, grad_hbm, *refs):
    packs, (disp_ref, comb_ref, sum_ref, param_ref) = list(refs[:seqs]), refs[seqs + 1 : seqs + 5]
    slot_ref, logit_ref, grad_ref, early_ref, sems = refs[seqs + 5 :]
    slots, width = logit_ref.shape[1], grad_ref.shape[1]
    early = [(packs[other], early_ref.at[other // 2]) for other in range(0, seqs, 2)]
    got_logits, *got_early, got_grad = fetch(
        [(logit_hbm, logit_ref)] + early + [(grad_hbm, grad_ref)], sems
    )
    got_logits.wait()
    scores = logit_ref[...].astype(jnp.float32)
    raised = jnp.exp(scores - jnp.max(scores, axis=1, keepdims=True))
    combine = raised / jnp.sum(raised, axis=1, keepdims=True)
    for other in range(0, seqs, 2):
        got_early[other // 2].wait()
        packs[other] = early_ref.at[other // 2]
    seq_slots = slots // seqs
    me = me_ref[0]
    stats = []
    for other, pack in enumerate(packs):
        base = slots + 2 * seq_slots
        rows = pack[base : base + stat_rows(slots, width)].astype(jnp.float32)
        parts = [
            jnp.concatenate([rows[r : r + 1, lane : lane + GROUP] for _, r, lane in places], axis=1)
            for places in stat_places(slots, width)
        ]
        stats.append((parts[0], parts[1] + parts[2] + parts[3]))
        at = pl.ds(pl.multiple_of((me ^ other) * seq_slots, seq_slots), seq_slots)
        param_ref[at, :] = pack[slots : slots + seq_slots]
        slot_ref[at, :] = pack[slots + seq_slots : slots + 2 * seq_slots]
    highest = functools.reduce(jnp.maximum, [top for top, _ in stats])
    total = sum(part * jnp.exp(top - highest) for top, part in stats)
    row = lax.broadcasted_iota(jnp.int32, (slots, slots), 0)
    col = lax.broadcasted_iota(jnp.int32, (slots, slots), 1)
    token_sum = jnp.zeros((slots, width), jnp.float32)
    for pack, (top, _) in zip(packs, stats):
        share = jnp.exp(top - highest) / total
        share = jnp.sum(jnp.where(row == col, share, 0.0), axis=1, keepdims=True)
        token_sum += share * pack[:slots].astype(jnp.float32)
    sum_ref[...] = token_sum.astype(jnp.bfloat16)
    disp_ref[...] = jnp.exp(scores - highest) / total
    got_grad.wait()
    comb_cot = dot_nt(grad_ref[...], slot_ref[...])
    comb_ref[...] = combine * (comb_cot - jnp.sum(combine * comb_cot, axis=1, keepdims=True))


def on_device(
    tokens, out_grad, saved_logits, slot_params, slot_inputs, slot_outputs, expert_in, expert_out
):
    clip_count = lax.axis_size("clip")
    seq_count = lax.axis_size("seq")
    device_count = clip_count * seq_count
    there, back = (exchange_order(device_count, *seed) for seed in SHUFFLES)
    tok_feats, out_cot, logit_raw = tokens[0], out_grad[0], saved_logits[0]
    token_total, width = tok_feats.shape
    slot_total = logit_raw.shape[1]
    clip_total, local_slots = slot_inputs.shape[:2]
    hid = expert_in.shape[2]
    feed_rows = clip_total * local_slots
    f32, b16 = jnp.float32, jnp.bfloat16

    still_logits, still_grad = stays(logit_raw), stays(out_cot)
    still_in, still_out = stays(expert_in[0]), stays(expert_out[0])
    blocks = pl.pallas_call(
        functools.partial(cot_kernel, there),
        out_shape=jax.ShapeDtypeStruct((device_count, local_slots, width), b16),
        in_specs=[STAYS, STAYS],
        out_specs=WHOLE,
        scratch_shapes=[
            pltpu.VMEM((token_total, slot_total), b16),
            pltpu.VMEM((token_total, width), b16),
            pltpu.SemaphoreType.DMA((2,)),
        ],
        compiler_params=pltpu.CompilerParams(vmem_limit_bytes=16 * MIB),
        cost_estimate=FREE,
    )(still_logits, still_grad)
    received = exchange(blocks, there)

    parts = math.gcd(hid // GROUP, 4)
    seq_slots = slot_params.shape[1]
    pack_rows = slot_total + 2 * seq_slots + stat_rows(slot_total, width)
    pieces = math.gcd(hid // GROUP, 6)
    chunk, wide = hid // pieces, hid // math.gcd(pieces, 3)
    kept_rows = max(pieces // 2, 1) * chunk
    own, slope, kept = pl.pallas_call(
        functools.partial(side_kernel, parts),
        out_shape=(
            jax.ShapeDtypeStruct((pack_rows, width), b16),
            jax.ShapeDtypeStruct((feed_rows, hid), b16),
            pltpu.VMEM((kept_rows, width), b16),
        ),
        in_specs=[STAYS] * 7,
        out_specs=(WHOLE,) * 3,
        scratch_shapes=[
            pltpu.VMEM((token_total, slot_total), b16),
            pltpu.VMEM((token_total, width), b16),
            pltpu.VMEM(slot_inputs.shape, b16),
            pltpu.VMEM((stat_rows(slot_total, width), width), f32),
            pltpu.VMEM((width, hid), b16),
            pltpu.SemaphoreType.DMA((6 + parts,)),
        ],
        compiler_params=pltpu.CompilerParams(vmem_limit_bytes=24 * MIB),
        cost_estimate=FREE,
    )(
        still_logits,
        stays(tok_feats),
        stays(slot_params.T),
        stays(slot_outputs[0]),
        stays(slot_inputs),
        still_in,
        still_out,
    )

    send = pl.pallas_call(
        functools.partial(expert_kernel, there, back, clip_count, seq_count, chunk, wide),
        out_shape=jax.ShapeDtypeStruct((device_count, local_slots, width), b16),
        in_specs=[WHOLE, WHOLE, WHOLE, STAYS, STAYS],
        out_specs=WHOLE,
        scratch_shapes=[
            pltpu.VMEM((width, hid), b16),
            pltpu.VMEM((max(hid - kept_rows, chunk), width), b16),
            pltpu.VMEM((feed_rows, hid), b16),
            pltpu.SemaphoreType.DMA(((hid - kept_rows) // chunk + hid // wide,)),
        ],
        compiler_params=pltpu.CompilerParams(vmem_limit_bytes=20 * MIB),
        cost_estimate=pl.CostEstimate(
            flops=4 * feed_rows * width * hid,
            bytes_accessed=4 * width * hid,
            transcendentals=0,
        ),
    )(
        received,
        pltpu.with_memory_space_constraint(kept, pltpu.VMEM),
        slope,
        still_in,
        still_out,
    )
    returned = exchange(send, back)

    held = {0: own}
    for bit in seq_bits():
        for other in list(held):
            held[other ^ bit] = swap(held[other] if other == 0 else after(held[other], send), bit)
    dispatch, comb_logit, token_sum, param_all = pl.pallas_call(
        functools.partial(weight_kernel, seq_count),
        out_shape=(
            jax.ShapeDtypeStruct((token_total, slot_total), f32),
            jax.ShapeDtypeStruct((token_total, slot_total), f32),
            jax.ShapeDtypeStruct((slot_total, width), b16),
            jax.ShapeDtypeStruct((slot_total, width), b16),
        ),
        in_specs=[pl.BlockSpec(memory_space=pltpu.SMEM), STAYS, STAYS]
        + [STAYS if other % 2 == 0 else WHOLE for other in range(seq_count)]
        + [PLACED],
        out_specs=(WHOLE,) * 4,
        scratch_shapes=[
            pltpu.VMEM((slot_total, width), b16),
            pltpu.VMEM((token_total, slot_total), b16),
            pltpu.VMEM((token_total, width), b16),
            pltpu.VMEM(((seq_count + 1) // 2, pack_rows, width), b16),
            pltpu.SemaphoreType.DMA((2 + (seq_count + 1) // 2,)),
        ],
        compiler_params=pltpu.CompilerParams(vmem_limit_bytes=48 * MIB),
        cost_estimate=FREE,
    )(
        lax.axis_index("seq")[None],
        still_logits,
        still_grad,
        *[stays(held[at]) if at % 2 == 0 else held[at] for at in range(seq_count)],
        send,
    )

    step = math.gcd(token_total, 128)
    token_grad = pl.pallas_call(
        functools.partial(token_kernel, back, step),
        out_shape=jax.ShapeDtypeStruct((token_total, width), b16),
        in_specs=[WHOLE] * 6,
        out_specs=PLACED,
        scratch_shapes=[
            pltpu.VMEM((token_total, width), b16),
            pltpu.SemaphoreType.DMA((token_total // step,)),
        ],
        compiler_params=pltpu.CompilerParams(vmem_limit_bytes=16 * MIB),
        cost_estimate=pl.CostEstimate(
            flops=6 * token_total * width * slot_total,
            bytes_accessed=4 * token_total * width,
            transcendentals=0,
        ),
    )(
        tok_feats,
        returned,
        token_sum,
        dispatch,
        comb_logit,
        param_all,
    )
    return token_grad[None]


def solution(mesh):
    placed = (
        P("clip", "seq", None),
        P("clip", "seq", None),
        P("clip", "seq", None),
        P(None, "seq"),
        P(None, BOTH, None),
        P("clip", "seq", None),
        P(BOTH, None, None),
        P(BOTH, None, None),
    )
    return jax.shard_map(
        on_device, mesh=mesh, in_specs=placed, out_specs=P("clip", "seq", None), check_vma=False
    )
```

```python
import functools
import math
import random
import jax
import jax.numpy as jnp
from jax import lax
from jax.experimental import pallas as pl
from jax.experimental.pallas import tpu as pltpu
from jax.sharding import PartitionSpec as P

BOTH = ("clip", "seq")
WHOLE = pl.BlockSpec(memory_space=pltpu.VMEM)
PLACED = pl.BlockSpec(memory_space=pl.ANY)
STAYS = pl.BlockSpec(memory_space=pltpu.HBM)
GROUP = 128
SHUFFLES = ((1, 25), (1, 12))
MIB = 1 << 20
FREE = pl.CostEstimate(flops=0, bytes_accessed=0, transcendentals=0)


def dot_nn(a, b):
    return jnp.dot(a, b, preferred_element_type=jnp.float32)


def dot_nt(a, b):
    return lax.dot_general(a, b, (((1,), (1,)), ((), ())), preferred_element_type=jnp.float32)


def dot_tn(a, b):
    return lax.dot_general(a, b, (((0,), (0,)), ((), ())), preferred_element_type=jnp.float32)


def exchange_order(devices, seed, turns):
    shuffler = random.Random(seed)
    for _ in range(turns):
        order = list(range(devices))
        shuffler.shuffle(order)
    return order


def exchange(blocks, order):
    return lax.all_to_all(
        blocks, BOTH, split_axis=0, concat_axis=0, axis_index_groups=[order], tiled=True
    )


def fetch(pairs, sems):
    copies = [
        pltpu.make_async_copy(source, held, sems.at[at]) for at, (source, held) in enumerate(pairs)
    ]
    for copy in copies:
        copy.start()
    return copies


def cot_kernel(order, logit_hbm, grad_hbm, out_ref, logit_ref, grad_ref, sems):
    got_logits, got_grad = fetch([(logit_hbm, logit_ref), (grad_hbm, grad_ref)], sems)
    got_logits.wait()
    scores = logit_ref[...].astype(jnp.float32)
    raised = jnp.exp(scores - jnp.max(scores, axis=1, keepdims=True))
    combine = raised / jnp.sum(raised, axis=1, keepdims=True)
    got_grad.wait()
    cot = dot_tn(combine.astype(jnp.bfloat16), grad_ref[...])
    cot = cot.reshape(out_ref.shape)
    for place, device in enumerate(order):
        out_ref[place] = cot[device].astype(jnp.bfloat16)


def expert_kernel(
    there, back, clips, seqs, chunk, wide, got_ref, kept_ref, slope_hbm, in_hbm, out_hbm, send_ref,
    slope_ref, in_ref, out_ref, act_ref, cot_ref, sems
):
    rows, width = got_ref.shape[1:]
    hid, kept = in_hbm.shape[1], kept_ref.shape[0]
    outs, ins = (hid - kept) // chunk, hid // wide

    def place(part, size, shift=0):
        return pl.ds(pl.multiple_of(shift + part * size, GROUP), size)

    def out_copy(part):
        return pltpu.make_async_copy(
            out_hbm.at[place(part, chunk, kept), :], out_ref.at[place(part, chunk), :], sems.at[part]
        )

    def in_copy(part):
        at = place(part, wide)
        return pltpu.make_async_copy(in_hbm.at[:, at], in_ref.at[:, at], sems.at[outs + part])

    slope_copy = pltpu.make_async_copy(slope_hbm, slope_ref, sems.at[outs + ins])
    slope_copy.start()
    for part in range(outs):
        out_copy(part).start()
    for part in range(ins):
        in_copy(part).start()
    got = [got_ref[there.index(device)].astype(jnp.float32) for device in range(clips * seqs)]
    cot = [sum(got[clip * seqs : (clip + 1) * seqs]) for clip in range(clips)]
    cot = jnp.concatenate(cot, axis=0).astype(jnp.bfloat16)

    @pl.loop(0, kept // chunk)
    def _(part):
        at = place(part, chunk)
        act_ref[:, at] = dot_nt(cot, kept_ref[at, :])

    slope_copy.wait()
    cot_ref[:, :kept] = (act_ref[...] * slope_ref[:, :kept]).astype(jnp.bfloat16)

    @pl.loop(0, outs)
    def _(part):
        out_copy(part).wait()
        at = place(part, chunk, kept)
        act_cot = dot_nt(cot, out_ref[place(part, chunk), :])
        cot_ref[:, at] = (act_cot * slope_ref[:, at]).astype(jnp.bfloat16)

    def add(part, total):
        in_copy(part).wait()
        at = place(part, wide)
        return total + dot_nt(cot_ref[:, at], in_ref[:, at])

    grad = lax.fori_loop(0, ins, add, jnp.zeros((clips * rows, width), jnp.float32))
    grad = grad.reshape(clips, rows, width).astype(jnp.bfloat16)
    for at, device in enumerate(back):
        send_ref[at] = grad[device // seqs]


def token_kernel(
    order, chunk, tok_ref, got_ref, sum_ref, disp_ref, comb_ref, param_ref,
    out_hbm, stage, sems
):
    slots = param_ref.shape[0]
    slot_grad = [got_ref[order.index(at)].astype(jnp.float32) for at in range(len(order))]
    slot_grad = jnp.concatenate(slot_grad, axis=0).astype(jnp.bfloat16)
    cross = dot_nt(sum_ref[...], slot_grad)
    halves = math.gcd(tok_ref.shape[0] // chunk, 2)
    half = tok_ref.shape[0] // halves
    disp_cot = [dot_nt(tok_ref[pl.ds(at * half, half), :], slot_grad) for at in range(halves)]
    disp_cot = jnp.concatenate(disp_cot, axis=0)
    row = lax.broadcasted_iota(jnp.int32, (slots, slots), 0)
    col = lax.broadcasted_iota(jnp.int32, (slots, slots), 1)
    slot_dots = jnp.sum(jnp.where(row == col, cross, 0.0), axis=0, keepdims=True)
    both_rows = jnp.concatenate([slot_grad, param_ref[...]], axis=0)
    copies = []
    for step in range(tok_ref.shape[0] // chunk):
        part = pl.ds(step * chunk, chunk)
        dispatch = disp_ref[part, :]
        logit_grad = comb_ref[part, :] + dispatch * (disp_cot[part.start : part.start + chunk] - slot_dots)
        weights = jnp.concatenate([dispatch, logit_grad], axis=1).astype(jnp.bfloat16)
        stage[part, :] = dot_nn(weights, both_rows).astype(jnp.bfloat16)
        copy = pltpu.make_async_copy(stage.at[part, :], out_hbm.at[part, :], sems.at[step])
        copy.start()
        copies.append(copy)
    for copy in copies:
        copy.wait()


def stays(value):
    return pltpu.with_memory_space_constraint(value, pltpu.HBM)


def after(value, token):
    return lax.optimization_barrier((value, token))[0]


def seq_bits():
    count = lax.axis_size("seq")
    return [1 << place for place in reversed(range(count.bit_length() - 1))]


def swap(value, bit):
    count = lax.axis_size("seq")
    return lax.ppermute(value, "seq", [(i, i ^ bit) for i in range(count)])


def stat_places(slots, width):
    groups, per_row = slots // GROUP, width // GROUP
    return [
        [(g * GROUP, (v * groups + g) // per_row, (v * groups + g) % per_row * GROUP) for g in range(groups)]
        for v in range(4)
    ]


def stat_rows(slots, width):
    return -(-4 * slots // (16 * width)) * 16


def side_kernel(
    parts, logit_hbm, tok_hbm, param_hbm, slot_hbm, feed_hbm, in_hbm, out_hbm,
    pack_ref, slope_ref, kept_ref, logit_ref, tok_ref, feed_ref, stat_ref, in_ref, sems
):
    slots, width = logit_ref.shape[1], tok_ref.shape[1]
    seq_slots = slot_hbm.shape[0]
    hid = in_hbm.shape[1]
    places = [pl.ds(part * (hid // parts), hid // parts) for part in range(parts)]
    copies = fetch(
        [
            (logit_hbm, logit_ref),
            (tok_hbm, tok_ref),
            (param_hbm, pack_ref.at[pl.ds(slots, seq_slots)]),
            (slot_hbm, pack_ref.at[pl.ds(slots + seq_slots, seq_slots)]),
            (feed_hbm, feed_ref),
        ]
        + [(in_hbm.at[:, at], in_ref.at[:, at]) for at in places]
        + [(out_hbm.at[pl.ds(0, kept_ref.shape[0])], kept_ref)],
        sems,
    )
    copies[0].wait()
    scores = logit_ref[...].astype(jnp.float32)
    highest = jnp.max(scores, axis=0, keepdims=True)
    raised = jnp.exp(scores - highest)
    total = jnp.sum(raised, axis=0, keepdims=True)
    part0 = total.astype(jnp.bfloat16).astype(jnp.float32)
    part1 = (total - part0).astype(jnp.bfloat16).astype(jnp.float32)
    part2 = total - part0 - part1
    stat_ref[...] = jnp.zeros_like(stat_ref)
    for vector, spots in zip((highest, part0, part1, part2), stat_places(slots, width)):
        for slot, row, lane in spots:
            stat_ref[row : row + 1, lane : lane + GROUP] = vector[:, slot : slot + GROUP]
    pack_ref[slots + 2 * seq_slots :] = stat_ref[...].astype(jnp.bfloat16)
    copies[1].wait()
    pack_ref[:slots] = dot_tn(raised.astype(jnp.bfloat16), tok_ref[...]).astype(jnp.bfloat16)
    copies[4].wait()
    feed = [feed_ref[clip].astype(jnp.float32) for clip in range(feed_ref.shape[0])]
    feed = jnp.concatenate(feed, axis=0).astype(jnp.bfloat16)
    root = math.sqrt(2.0 / math.pi)
    for at, copy in zip(places, copies[5:]):
        copy.wait()
        x = dot_nn(feed, in_ref[:, at])
        bend = jnp.tanh(root * (x + 0.044715 * (x * x * x)))
        grown = root * (1.0 + 3.0 * 0.044715 * (x * x))
        slope_ref[:, at] = 0.5 * (1.0 + bend) + 0.5 * x * (1.0 - bend * bend) * grown
    copies[2].wait()
    copies[3].wait()
    copies[-1].wait()


def weight_kernel(seqs, me_ref, logit_hbm, grad_hbm, *refs):
    packs, (disp_ref, comb_ref, sum_ref, param_ref) = list(refs[:seqs]), refs[seqs + 1 : seqs + 5]
    slot_ref, logit_ref, grad_ref, early_ref, sems = refs[seqs + 5 :]
    slots, width = logit_ref.shape[1], grad_ref.shape[1]
    early = [(packs[other], early_ref.at[other // 2]) for other in range(0, seqs, 2)]
    got_logits, *got_early, got_grad = fetch(
        [(logit_hbm, logit_ref)] + early + [(grad_hbm, grad_ref)], sems
    )
    got_logits.wait()
    scores = logit_ref[...].astype(jnp.float32)
    raised = jnp.exp(scores - jnp.max(scores, axis=1, keepdims=True))
    combine = raised / jnp.sum(raised, axis=1, keepdims=True)
    for other in range(0, seqs, 2):
        got_early[other // 2].wait()
        packs[other] = early_ref.at[other // 2]
    seq_slots = slots // seqs
    me = me_ref[0]
    stats = []
    for other, pack in enumerate(packs):
        base = slots + 2 * seq_slots
        rows = pack[base : base + stat_rows(slots, width)].astype(jnp.float32)
        parts = [
            jnp.concatenate([rows[r : r + 1, lane : lane + GROUP] for _, r, lane in places], axis=1)
            for places in stat_places(slots, width)
        ]
        stats.append((parts[0], parts[1] + parts[2] + parts[3]))
        at = pl.ds(pl.multiple_of((me ^ other) * seq_slots, seq_slots), seq_slots)
        param_ref[at, :] = pack[slots : slots + seq_slots]
        slot_ref[at, :] = pack[slots + seq_slots : slots + 2 * seq_slots]
    highest = functools.reduce(jnp.maximum, [top for top, _ in stats])
    total = sum(part * jnp.exp(top - highest) for top, part in stats)
    row = lax.broadcasted_iota(jnp.int32, (slots, slots), 0)
    col = lax.broadcasted_iota(jnp.int32, (slots, slots), 1)
    token_sum = jnp.zeros((slots, width), jnp.float32)
    for pack, (top, _) in zip(packs, stats):
        share = jnp.exp(top - highest) / total
        share = jnp.sum(jnp.where(row == col, share, 0.0), axis=1, keepdims=True)
        token_sum += share * pack[:slots].astype(jnp.float32)
    sum_ref[...] = token_sum.astype(jnp.bfloat16)
    disp_ref[...] = jnp.exp(scores - highest) / total
    got_grad.wait()
    comb_cot = dot_nt(grad_ref[...], slot_ref[...])
    comb_ref[...] = combine * (comb_cot - jnp.sum(combine * comb_cot, axis=1, keepdims=True))


def on_device(
    tokens, out_grad, saved_logits, slot_params, slot_inputs, slot_outputs, expert_in, expert_out
):
    clip_count = lax.axis_size("clip")
    seq_count = lax.axis_size("seq")
    device_count = clip_count * seq_count
    there, back = (exchange_order(device_count, *seed) for seed in SHUFFLES)
    tok_feats, out_cot, logit_raw = tokens[0], out_grad[0], saved_logits[0]
    token_total, width = tok_feats.shape
    slot_total = logit_raw.shape[1]
    clip_total, local_slots = slot_inputs.shape[:2]
    hid = expert_in.shape[2]
    feed_rows = clip_total * local_slots
    f32, b16 = jnp.float32, jnp.bfloat16

    still_logits, still_grad = stays(logit_raw), stays(out_cot)
    still_in, still_out = stays(expert_in[0]), stays(expert_out[0])
    blocks = pl.pallas_call(
        functools.partial(cot_kernel, there),
        out_shape=jax.ShapeDtypeStruct((device_count, local_slots, width), b16),
        in_specs=[STAYS, STAYS],
        out_specs=WHOLE,
        scratch_shapes=[
            pltpu.VMEM((token_total, slot_total), b16),
            pltpu.VMEM((token_total, width), b16),
            pltpu.SemaphoreType.DMA((2,)),
        ],
        compiler_params=pltpu.CompilerParams(vmem_limit_bytes=16 * MIB),
        cost_estimate=FREE,
    )(still_logits, still_grad)
    received = exchange(blocks, there)

    parts = math.gcd(hid // GROUP, 4)
    seq_slots = slot_params.shape[1]
    pack_rows = slot_total + 2 * seq_slots + stat_rows(slot_total, width)
    pieces = math.gcd(hid // GROUP, 6)
    chunk, wide = hid // pieces, hid // math.gcd(pieces, 3)
    kept_rows = max(pieces // 2, 1) * chunk
    own, slope, kept = pl.pallas_call(
        functools.partial(side_kernel, parts),
        out_shape=(
            jax.ShapeDtypeStruct((pack_rows, width), b16),
            pltpu.HBM((feed_rows, hid), f32),
            pltpu.VMEM((kept_rows, width), b16),
        ),
        in_specs=[STAYS] * 7,
        out_specs=(WHOLE,) * 3,
        scratch_shapes=[
            pltpu.VMEM((token_total, slot_total), b16),
            pltpu.VMEM((token_total, width), b16),
            pltpu.VMEM(slot_inputs.shape, b16),
            pltpu.VMEM((stat_rows(slot_total, width), width), f32),
            pltpu.VMEM((width, hid), b16),
            pltpu.SemaphoreType.DMA((6 + parts,)),
        ],
        compiler_params=pltpu.CompilerParams(vmem_limit_bytes=24 * MIB),
        cost_estimate=FREE,
    )(
        still_logits,
        stays(tok_feats),
        stays(slot_params.T),
        stays(slot_outputs[0]),
        stays(slot_inputs),
        still_in,
        still_out,
    )

    send = pl.pallas_call(
        functools.partial(expert_kernel, there, back, clip_count, seq_count, chunk, wide),
        out_shape=jax.ShapeDtypeStruct((device_count, local_slots, width), b16),
        in_specs=[WHOLE, WHOLE, STAYS, STAYS, STAYS],
        out_specs=WHOLE,
        scratch_shapes=[
            pltpu.VMEM((feed_rows, hid), f32),
            pltpu.VMEM((width, hid), b16),
            pltpu.VMEM((max(hid - kept_rows, chunk), width), b16),
            pltpu.VMEM((feed_rows, kept_rows), f32),
            pltpu.VMEM((feed_rows, hid), b16),
            pltpu.SemaphoreType.DMA(((hid - kept_rows) // chunk + hid // wide + 1,)),
        ],
        compiler_params=pltpu.CompilerParams(vmem_limit_bytes=20 * MIB),
        cost_estimate=pl.CostEstimate(
            flops=4 * feed_rows * width * hid,
            bytes_accessed=4 * width * hid,
            transcendentals=0,
        ),
    )(
        received,
        pltpu.with_memory_space_constraint(kept, pltpu.VMEM),
        stays(slope),
        still_in,
        still_out,
    )
    returned = exchange(send, back)

    held = {0: own}
    for bit in seq_bits():
        for other in list(held):
            held[other ^ bit] = swap(held[other] if other == 0 else after(held[other], send), bit)
    dispatch, comb_logit, token_sum, param_all = pl.pallas_call(
        functools.partial(weight_kernel, seq_count),
        out_shape=(
            jax.ShapeDtypeStruct((token_total, slot_total), f32),
            jax.ShapeDtypeStruct((token_total, slot_total), f32),
            jax.ShapeDtypeStruct((slot_total, width), b16),
            jax.ShapeDtypeStruct((slot_total, width), b16),
        ),
        in_specs=[pl.BlockSpec(memory_space=pltpu.SMEM), STAYS, STAYS]
        + [STAYS if other % 2 == 0 else WHOLE for other in range(seq_count)]
        + [PLACED],
        out_specs=(WHOLE,) * 4,
        scratch_shapes=[
            pltpu.VMEM((slot_total, width), b16),
            pltpu.VMEM((token_total, slot_total), b16),
            pltpu.VMEM((token_total, width), b16),
            pltpu.VMEM(((seq_count + 1) // 2, pack_rows, width), b16),
            pltpu.SemaphoreType.DMA((2 + (seq_count + 1) // 2,)),
        ],
        compiler_params=pltpu.CompilerParams(vmem_limit_bytes=48 * MIB),
        cost_estimate=FREE,
    )(
        lax.axis_index("seq")[None],
        still_logits,
        still_grad,
        *[stays(held[at]) if at % 2 == 0 else held[at] for at in range(seq_count)],
        send,
    )

    step = math.gcd(token_total, 128)
    token_grad = pl.pallas_call(
        functools.partial(token_kernel, back, step),
        out_shape=jax.ShapeDtypeStruct((token_total, width), b16),
        in_specs=[WHOLE] * 6,
        out_specs=PLACED,
        scratch_shapes=[
            pltpu.VMEM((token_total, width), b16),
            pltpu.SemaphoreType.DMA((token_total // step,)),
        ],
        compiler_params=pltpu.CompilerParams(vmem_limit_bytes=16 * MIB),
        cost_estimate=pl.CostEstimate(
            flops=6 * token_total * width * slot_total,
            bytes_accessed=4 * token_total * width,
            transcendentals=0,
        ),
    )(
        tok_feats,
        returned,
        token_sum,
        dispatch,
        comb_logit,
        param_all,
    )
    return token_grad[None]


def solution(mesh):
    placed = (
        P("clip", "seq", None),
        P("clip", "seq", None),
        P("clip", "seq", None),
        P(None, "seq"),
        P(None, BOTH, None),
        P("clip", "seq", None),
        P(BOTH, None, None),
        P(BOTH, None, None),
    )
    return jax.shard_map(
        on_device, mesh=mesh, in_specs=placed, out_specs=P("clip", "seq", None), check_vma=False
    )
```

```python
import functools
import math
import random
import jax
import jax.numpy as jnp
from jax import lax
from jax.experimental import pallas as pl
from jax.experimental.pallas import tpu as pltpu
from jax.sharding import PartitionSpec as P

BOTH = ("clip", "seq")
WHOLE = pl.BlockSpec(memory_space=pltpu.VMEM)
PLACED = pl.BlockSpec(memory_space=pl.ANY)
STAYS = pl.BlockSpec(memory_space=pltpu.HBM)
GROUP = 128
SHUFFLES = ((1, 25), (1, 12))
MIB = 1 << 20
FREE = pl.CostEstimate(flops=0, bytes_accessed=0, transcendentals=0)


def dot_nn(a, b):
    return jnp.dot(a, b, preferred_element_type=jnp.float32)


def dot_nt(a, b):
    return lax.dot_general(a, b, (((1,), (1,)), ((), ())), preferred_element_type=jnp.float32)


def dot_tn(a, b):
    return lax.dot_general(a, b, (((0,), (0,)), ((), ())), preferred_element_type=jnp.float32)


def exchange_order(devices, seed, turns):
    shuffler = random.Random(seed)
    for _ in range(turns):
        order = list(range(devices))
        shuffler.shuffle(order)
    return order


def exchange(blocks, order):
    return lax.all_to_all(
        blocks, BOTH, split_axis=0, concat_axis=0, axis_index_groups=[order], tiled=True
    )


def fetch(pairs, sems):
    copies = [
        pltpu.make_async_copy(source, held, sems.at[at]) for at, (source, held) in enumerate(pairs)
    ]
    for copy in copies:
        copy.start()
    return copies


def cot_kernel(order, logit_hbm, grad_hbm, out_ref, logit_ref, grad_ref, sems):
    got_logits, got_grad = fetch([(logit_hbm, logit_ref), (grad_hbm, grad_ref)], sems)
    got_logits.wait()
    scores = logit_ref[...].astype(jnp.float32)
    raised = jnp.exp(scores - jnp.max(scores, axis=1, keepdims=True))
    combine = raised / jnp.sum(raised, axis=1, keepdims=True)
    got_grad.wait()
    cot = dot_tn(combine.astype(jnp.bfloat16), grad_ref[...])
    cot = cot.reshape(out_ref.shape)
    for place, device in enumerate(order):
        out_ref[place] = cot[device].astype(jnp.bfloat16)


def expert_kernel(
    there, back, clips, seqs, chunk, wide, got_ref, kept_ref, slope_ref, in_hbm, out_hbm, send_ref,
    in_ref, out_ref, cot_ref, sems
):
    rows, width = got_ref.shape[1:]
    hid, kept = in_hbm.shape[1], kept_ref.shape[0]
    outs, ins = (hid - kept) // chunk, hid // wide

    def place(part, size, shift=0):
        return pl.ds(pl.multiple_of(shift + part * size, GROUP), size)

    def out_copy(part):
        return pltpu.make_async_copy(
            out_hbm.at[place(part, chunk, kept), :], out_ref.at[place(part, chunk), :], sems.at[part]
        )

    def in_copy(part):
        at = place(part, wide)
        return pltpu.make_async_copy(in_hbm.at[:, at], in_ref.at[:, at], sems.at[outs + part])

    for part in range(outs):
        out_copy(part).start()
    for part in range(ins):
        in_copy(part).start()
    got = [got_ref[there.index(device)].astype(jnp.float32) for device in range(clips * seqs)]
    cot = [sum(got[clip * seqs : (clip + 1) * seqs]) for clip in range(clips)]
    cot = jnp.concatenate(cot, axis=0).astype(jnp.bfloat16)

    @pl.loop(0, kept // chunk)
    def _(part):
        at = place(part, chunk)
        cot_ref[:, at] = (dot_nt(cot, kept_ref[at, :]) * slope_ref[:, at]).astype(jnp.bfloat16)

    @pl.loop(0, outs)
    def _(part):
        out_copy(part).wait()
        at = place(part, chunk, kept)
        act_cot = dot_nt(cot, out_ref[place(part, chunk), :])
        cot_ref[:, at] = (act_cot * slope_ref[:, at]).astype(jnp.bfloat16)

    def add(part, total):
        in_copy(part).wait()
        at = place(part, wide)
        return total + dot_nt(cot_ref[:, at], in_ref[:, at])

    grad = lax.fori_loop(0, ins, add, jnp.zeros((clips * rows, width), jnp.float32))
    grad = grad.reshape(clips, rows, width).astype(jnp.bfloat16)
    for at, device in enumerate(back):
        send_ref[at] = grad[device // seqs]


def token_kernel(
    order, chunk, tok_ref, got_ref, sum_ref, disp_ref, comb_ref, param_ref,
    out_hbm, stage, sems
):
    slots = param_ref.shape[0]
    slot_grad = [got_ref[order.index(at)].astype(jnp.float32) for at in range(len(order))]
    slot_grad = jnp.concatenate(slot_grad, axis=0).astype(jnp.bfloat16)
    cross = dot_nt(sum_ref[...], slot_grad)
    halves = math.gcd(tok_ref.shape[0] // chunk, 2)
    half = tok_ref.shape[0] // halves
    disp_cot = [dot_nt(tok_ref[pl.ds(at * half, half), :], slot_grad) for at in range(halves)]
    disp_cot = jnp.concatenate(disp_cot, axis=0)
    row = lax.broadcasted_iota(jnp.int32, (slots, slots), 0)
    col = lax.broadcasted_iota(jnp.int32, (slots, slots), 1)
    slot_dots = jnp.sum(jnp.where(row == col, cross, 0.0), axis=0, keepdims=True)
    both_rows = jnp.concatenate([slot_grad, param_ref[...]], axis=0)
    copies = []
    for step in range(tok_ref.shape[0] // chunk):
        part = pl.ds(step * chunk, chunk)
        dispatch = disp_ref[part, :]
        logit_grad = comb_ref[part, :] + dispatch * (disp_cot[part.start : part.start + chunk] - slot_dots)
        weights = jnp.concatenate([dispatch, logit_grad], axis=1).astype(jnp.bfloat16)
        stage[part, :] = dot_nn(weights, both_rows).astype(jnp.bfloat16)
        copy = pltpu.make_async_copy(stage.at[part, :], out_hbm.at[part, :], sems.at[step])
        copy.start()
        copies.append(copy)
    for copy in copies:
        copy.wait()


def stays(value):
    return pltpu.with_memory_space_constraint(value, pltpu.HBM)


def after(value, token):
    return lax.optimization_barrier((value, token))[0]


def seq_bits():
    count = lax.axis_size("seq")
    return [1 << place for place in reversed(range(count.bit_length() - 1))]


def swap(value, bit):
    count = lax.axis_size("seq")
    return lax.ppermute(value, "seq", [(i, i ^ bit) for i in range(count)])


def stat_places(slots, width):
    groups, per_row = slots // GROUP, width // GROUP
    return [
        [(g * GROUP, (v * groups + g) // per_row, (v * groups + g) % per_row * GROUP) for g in range(groups)]
        for v in range(4)
    ]


def stat_rows(slots, width):
    return -(-4 * slots // (16 * width)) * 16


def side_kernel(
    parts, logit_hbm, tok_hbm, param_hbm, slot_hbm, feed_hbm, in_hbm, out_hbm,
    pack_ref, slope_ref, kept_ref, logit_ref, tok_ref, feed_ref, stat_ref, in_ref, sems
):
    slots, width = logit_ref.shape[1], tok_ref.shape[1]
    seq_slots = slot_hbm.shape[0]
    hid = in_hbm.shape[1]
    places = [pl.ds(part * (hid // parts), hid // parts) for part in range(parts)]
    copies = fetch(
        [
            (logit_hbm, logit_ref),
            (tok_hbm, tok_ref),
            (param_hbm, pack_ref.at[pl.ds(slots, seq_slots)]),
            (slot_hbm, pack_ref.at[pl.ds(slots + seq_slots, seq_slots)]),
            (feed_hbm, feed_ref),
        ]
        + [(in_hbm.at[:, at], in_ref.at[:, at]) for at in places]
        + [(out_hbm.at[pl.ds(0, kept_ref.shape[0])], kept_ref)],
        sems,
    )
    copies[0].wait()
    scores = logit_ref[...].astype(jnp.float32)
    highest = jnp.max(scores, axis=0, keepdims=True)
    raised = jnp.exp(scores - highest)
    total = jnp.sum(raised, axis=0, keepdims=True)
    part0 = total.astype(jnp.bfloat16).astype(jnp.float32)
    part1 = (total - part0).astype(jnp.bfloat16).astype(jnp.float32)
    part2 = total - part0 - part1
    stat_ref[...] = jnp.zeros_like(stat_ref)
    for vector, spots in zip((highest, part0, part1, part2), stat_places(slots, width)):
        for slot, row, lane in spots:
            stat_ref[row : row + 1, lane : lane + GROUP] = vector[:, slot : slot + GROUP]
    pack_ref[slots + 2 * seq_slots :] = stat_ref[...].astype(jnp.bfloat16)
    copies[1].wait()
    pack_ref[:slots] = dot_tn(raised.astype(jnp.bfloat16), tok_ref[...]).astype(jnp.bfloat16)
    copies[4].wait()
    feed = [feed_ref[clip].astype(jnp.float32) for clip in range(feed_ref.shape[0])]
    feed = jnp.concatenate(feed, axis=0).astype(jnp.bfloat16)
    root = math.sqrt(2.0 / math.pi)
    for at, copy in zip(places, copies[5:]):
        copy.wait()
        x = dot_nn(feed, in_ref[:, at])
        bend = jnp.tanh(root * (x + 0.044715 * (x * x * x)))
        grown = root * (1.0 + 3.0 * 0.044715 * (x * x))
        slope = 0.5 * (1.0 + bend) + 0.5 * x * (1.0 - bend * bend) * grown
        slope_ref[:, at] = slope.astype(slope_ref.dtype)
    copies[2].wait()
    copies[3].wait()
    copies[-1].wait()


def weight_kernel(seqs, me_ref, logit_hbm, grad_hbm, *refs):
    packs, (disp_ref, comb_ref, sum_ref, param_ref) = list(refs[:seqs]), refs[seqs + 1 : seqs + 5]
    slot_ref, logit_ref, grad_ref, early_ref, sems = refs[seqs + 5 :]
    slots, width = logit_ref.shape[1], grad_ref.shape[1]
    early = [(packs[other], early_ref.at[other // 2]) for other in range(0, seqs, 2)]
    got_logits, *got_early, got_grad = fetch(
        [(logit_hbm, logit_ref)] + early + [(grad_hbm, grad_ref)], sems
    )
    got_logits.wait()
    scores = logit_ref[...].astype(jnp.float32)
    raised = jnp.exp(scores - jnp.max(scores, axis=1, keepdims=True))
    combine = raised / jnp.sum(raised, axis=1, keepdims=True)
    for other in range(0, seqs, 2):
        got_early[other // 2].wait()
        packs[other] = early_ref.at[other // 2]
    seq_slots = slots // seqs
    me = me_ref[0]
    stats = []
    for other, pack in enumerate(packs):
        base = slots + 2 * seq_slots
        rows = pack[base : base + stat_rows(slots, width)].astype(jnp.float32)
        parts = [
            jnp.concatenate([rows[r : r + 1, lane : lane + GROUP] for _, r, lane in places], axis=1)
            for places in stat_places(slots, width)
        ]
        stats.append((parts[0], parts[1] + parts[2] + parts[3]))
        at = pl.ds(pl.multiple_of((me ^ other) * seq_slots, seq_slots), seq_slots)
        param_ref[at, :] = pack[slots : slots + seq_slots]
        slot_ref[at, :] = pack[slots + seq_slots : slots + 2 * seq_slots]
    highest = functools.reduce(jnp.maximum, [top for top, _ in stats])
    total = sum(part * jnp.exp(top - highest) for top, part in stats)
    row = lax.broadcasted_iota(jnp.int32, (slots, slots), 0)
    col = lax.broadcasted_iota(jnp.int32, (slots, slots), 1)
    token_sum = jnp.zeros((slots, width), jnp.float32)
    for pack, (top, _) in zip(packs, stats):
        share = jnp.exp(top - highest) / total
        share = jnp.sum(jnp.where(row == col, share, 0.0), axis=1, keepdims=True)
        token_sum += share * pack[:slots].astype(jnp.float32)
    sum_ref[...] = token_sum.astype(jnp.bfloat16)
    disp_ref[...] = jnp.exp(scores - highest) / total
    got_grad.wait()
    comb_cot = dot_nt(grad_ref[...], slot_ref[...])
    comb_ref[...] = combine * (comb_cot - jnp.sum(combine * comb_cot, axis=1, keepdims=True))


def on_device(
    tokens, out_grad, saved_logits, slot_params, slot_inputs, slot_outputs, expert_in, expert_out
):
    clip_count = lax.axis_size("clip")
    seq_count = lax.axis_size("seq")
    device_count = clip_count * seq_count
    there, back = (exchange_order(device_count, *seed) for seed in SHUFFLES)
    tok_feats, out_cot, logit_raw = tokens[0], out_grad[0], saved_logits[0]
    token_total, width = tok_feats.shape
    slot_total = logit_raw.shape[1]
    clip_total, local_slots = slot_inputs.shape[:2]
    hid = expert_in.shape[2]
    feed_rows = clip_total * local_slots
    f32, b16 = jnp.float32, jnp.bfloat16

    still_logits, still_grad = stays(logit_raw), stays(out_cot)
    still_in, still_out = stays(expert_in[0]), stays(expert_out[0])
    blocks = pl.pallas_call(
        functools.partial(cot_kernel, there),
        out_shape=jax.ShapeDtypeStruct((device_count, local_slots, width), b16),
        in_specs=[STAYS, STAYS],
        out_specs=WHOLE,
        scratch_shapes=[
            pltpu.VMEM((token_total, slot_total), b16),
            pltpu.VMEM((token_total, width), b16),
            pltpu.SemaphoreType.DMA((2,)),
        ],
        compiler_params=pltpu.CompilerParams(vmem_limit_bytes=16 * MIB),
        cost_estimate=FREE,
    )(still_logits, still_grad)
    received = exchange(blocks, there)

    parts = math.gcd(hid // GROUP, 4)
    seq_slots = slot_params.shape[1]
    pack_rows = slot_total + 2 * seq_slots + stat_rows(slot_total, width)
    pieces = math.gcd(hid // GROUP, 6)
    chunk, wide = hid // pieces, hid // math.gcd(pieces, 3)
    kept_rows = max(pieces // 2, 1) * chunk
    own, slope, kept = pl.pallas_call(
        functools.partial(side_kernel, parts),
        out_shape=(
            jax.ShapeDtypeStruct((pack_rows, width), b16),
            jax.ShapeDtypeStruct((feed_rows, hid), b16),
            pltpu.VMEM((kept_rows, width), b16),
        ),
        in_specs=[STAYS] * 7,
        out_specs=(WHOLE,) * 3,
        scratch_shapes=[
            pltpu.VMEM((token_total, slot_total), b16),
            pltpu.VMEM((token_total, width), b16),
            pltpu.VMEM(slot_inputs.shape, b16),
            pltpu.VMEM((stat_rows(slot_total, width), width), f32),
            pltpu.VMEM((width, hid), b16),
            pltpu.SemaphoreType.DMA((6 + parts,)),
        ],
        compiler_params=pltpu.CompilerParams(vmem_limit_bytes=24 * MIB),
        cost_estimate=FREE,
    )(
        still_logits,
        stays(tok_feats),
        stays(slot_params.T),
        stays(slot_outputs[0]),
        stays(slot_inputs),
        still_in,
        still_out,
    )

    send = pl.pallas_call(
        functools.partial(expert_kernel, there, back, clip_count, seq_count, chunk, wide),
        out_shape=jax.ShapeDtypeStruct((device_count, local_slots, width), b16),
        in_specs=[WHOLE, WHOLE, WHOLE, STAYS, STAYS],
        out_specs=WHOLE,
        scratch_shapes=[
            pltpu.VMEM((width, hid), b16),
            pltpu.VMEM((max(hid - kept_rows, chunk), width), b16),
            pltpu.VMEM((feed_rows, hid), b16),
            pltpu.SemaphoreType.DMA(((hid - kept_rows) // chunk + hid // wide,)),
        ],
        compiler_params=pltpu.CompilerParams(vmem_limit_bytes=20 * MIB),
        cost_estimate=pl.CostEstimate(
            flops=4 * feed_rows * width * hid,
            bytes_accessed=4 * width * hid,
            transcendentals=0,
        ),
    )(
        received,
        pltpu.with_memory_space_constraint(kept, pltpu.VMEM),
        slope,
        still_in,
        still_out,
    )
    returned = exchange(send, back)

    held = {0: own}
    for bit in seq_bits():
        for other in list(held):
            held[other ^ bit] = swap(held[other] if other == 0 else after(held[other], send), bit)
    dispatch, comb_logit, token_sum, param_all = pl.pallas_call(
        functools.partial(weight_kernel, seq_count),
        out_shape=(
            jax.ShapeDtypeStruct((token_total, slot_total), f32),
            jax.ShapeDtypeStruct((token_total, slot_total), f32),
            jax.ShapeDtypeStruct((slot_total, width), b16),
            jax.ShapeDtypeStruct((slot_total, width), b16),
        ),
        in_specs=[pl.BlockSpec(memory_space=pltpu.SMEM), STAYS, STAYS]
        + [STAYS if other % 2 == 0 else WHOLE for other in range(seq_count)]
        + [PLACED],
        out_specs=(WHOLE,) * 4,
        scratch_shapes=[
            pltpu.VMEM((slot_total, width), b16),
            pltpu.VMEM((token_total, slot_total), b16),
            pltpu.VMEM((token_total, width), b16),
            pltpu.VMEM(((seq_count + 1) // 2, pack_rows, width), b16),
            pltpu.SemaphoreType.DMA((2 + (seq_count + 1) // 2,)),
        ],
        compiler_params=pltpu.CompilerParams(vmem_limit_bytes=48 * MIB),
        cost_estimate=FREE,
    )(
        lax.axis_index("seq")[None],
        still_logits,
        still_grad,
        *[stays(held[at]) if at % 2 == 0 else held[at] for at in range(seq_count)],
        send,
    )

    step = math.gcd(token_total, 128)
    token_grad = pl.pallas_call(
        functools.partial(token_kernel, back, step),
        out_shape=jax.ShapeDtypeStruct((token_total, width), b16),
        in_specs=[WHOLE] * 6,
        out_specs=PLACED,
        scratch_shapes=[
            pltpu.VMEM((token_total, width), b16),
            pltpu.SemaphoreType.DMA((token_total // step,)),
        ],
        compiler_params=pltpu.CompilerParams(vmem_limit_bytes=16 * MIB),
        cost_estimate=pl.CostEstimate(
            flops=6 * token_total * width * slot_total,
            bytes_accessed=4 * token_total * width,
            transcendentals=0,
        ),
    )(
        tok_feats,
        returned,
        token_sum,
        dispatch,
        comb_logit,
        param_all,
    )
    return token_grad[None]


def solution(mesh):
    placed = (
        P("clip", "seq", None),
        P("clip", "seq", None),
        P("clip", "seq", None),
        P(None, "seq"),
        P(None, BOTH, None),
        P("clip", "seq", None),
        P(BOTH, None, None),
        P(BOTH, None, None),
    )
    return jax.shard_map(
        on_device, mesh=mesh, in_specs=placed, out_specs=P("clip", "seq", None), check_vma=False
    )
```

```python
import functools
import math
import random
import jax
import jax.numpy as jnp
from jax import lax
from jax.experimental import pallas as pl
from jax.experimental.pallas import tpu as pltpu
from jax.sharding import PartitionSpec as P

BOTH = ("clip", "seq")
WHOLE = pl.BlockSpec(memory_space=pltpu.VMEM)
PLACED = pl.BlockSpec(memory_space=pl.ANY)
STAYS = pl.BlockSpec(memory_space=pltpu.HBM)
GROUP = 128
SHUFFLES = ((1, 25), (1, 12))
MIB = 1 << 20
FREE = pl.CostEstimate(flops=0, bytes_accessed=0, transcendentals=0)


def dot_nn(a, b):
    return jnp.dot(a, b, preferred_element_type=jnp.float32)


def dot_nt(a, b):
    return lax.dot_general(a, b, (((1,), (1,)), ((), ())), preferred_element_type=jnp.float32)


def dot_tn(a, b):
    return lax.dot_general(a, b, (((0,), (0,)), ((), ())), preferred_element_type=jnp.float32)


def exchange_order(devices, seed, turns):
    shuffler = random.Random(seed)
    for _ in range(turns):
        order = list(range(devices))
        shuffler.shuffle(order)
    return order


def exchange(blocks, order):
    return lax.all_to_all(
        blocks, BOTH, split_axis=0, concat_axis=0, axis_index_groups=[order], tiled=True
    )


def fetch(pairs, sems):
    copies = [
        pltpu.make_async_copy(source, held, sems.at[at]) for at, (source, held) in enumerate(pairs)
    ]
    for copy in copies:
        copy.start()
    return copies


def cot_kernel(order, logit_hbm, grad_hbm, out_ref, logit_ref, grad_ref, sems):
    got_logits, got_grad = fetch([(logit_hbm, logit_ref), (grad_hbm, grad_ref)], sems)
    got_logits.wait()
    scores = logit_ref[...].astype(jnp.float32)
    raised = jnp.exp(scores - jnp.max(scores, axis=1, keepdims=True))
    combine = raised / jnp.sum(raised, axis=1, keepdims=True)
    got_grad.wait()
    cot = dot_tn(combine.astype(jnp.bfloat16), grad_ref[...])
    cot = cot.reshape(out_ref.shape)
    for place, device in enumerate(order):
        out_ref[place] = cot[device].astype(jnp.bfloat16)


def expert_kernel(
    there, back, clips, seqs, chunk, wide, got_ref, kept_ref, slope_ref, in_hbm, out_hbm, send_ref,
    in_ref, out_ref, cot_ref, sems
):
    rows, width = got_ref.shape[1:]
    hid, kept = in_hbm.shape[1], kept_ref.shape[0]
    outs, ins = (hid - kept) // chunk, hid // wide

    def place(part, size, shift=0):
        return pl.ds(pl.multiple_of(shift + part * size, GROUP), size)

    def out_copy(part):
        return pltpu.make_async_copy(
            out_hbm.at[place(part, chunk, kept), :], out_ref.at[place(part, chunk), :], sems.at[part]
        )

    def in_copy(part):
        at = place(part, wide)
        return pltpu.make_async_copy(in_hbm.at[:, at], in_ref.at[:, at], sems.at[outs + part])

    for part in range(outs):
        out_copy(part).start()
    for part in range(ins):
        in_copy(part).start()
    got = [got_ref[there.index(device)].astype(jnp.float32) for device in range(clips * seqs)]
    cot = [sum(got[clip * seqs : (clip + 1) * seqs]) for clip in range(clips)]
    cot = jnp.concatenate(cot, axis=0).astype(jnp.bfloat16)

    @pl.loop(0, kept // chunk)
    def _(part):
        at = place(part, chunk)
        cot_ref[:, at] = (dot_nt(cot, kept_ref[at, :]) * slope_ref[:, at]).astype(jnp.bfloat16)

    @pl.loop(0, outs)
    def _(part):
        out_copy(part).wait()
        at = place(part, chunk, kept)
        act_cot = dot_nt(cot, out_ref[place(part, chunk), :])
        cot_ref[:, at] = (act_cot * slope_ref[:, at]).astype(jnp.bfloat16)

    def add(part, total):
        in_copy(part).wait()
        at = place(part, wide)
        return total + dot_nt(cot_ref[:, at], in_ref[:, at])

    grad = lax.fori_loop(0, ins, add, jnp.zeros((clips * rows, width), jnp.float32))
    grad = grad.reshape(clips, rows, width).astype(jnp.bfloat16)
    for at, device in enumerate(back):
        send_ref[at] = grad[device // seqs]


def token_kernel(
    order, chunk, tok_ref, got_ref, sum_ref, disp_ref, comb_ref, param_ref,
    out_hbm, stage, sems
):
    slots = param_ref.shape[0]
    slot_grad = [got_ref[order.index(at)].astype(jnp.float32) for at in range(len(order))]
    slot_grad = jnp.concatenate(slot_grad, axis=0).astype(jnp.bfloat16)
    cross = dot_nt(sum_ref[...], slot_grad)
    halves = math.gcd(tok_ref.shape[0] // chunk, 2)
    half = tok_ref.shape[0] // halves
    disp_cot = [dot_nt(tok_ref[pl.ds(at * half, half), :], slot_grad) for at in range(halves)]
    disp_cot = jnp.concatenate(disp_cot, axis=0)
    row = lax.broadcasted_iota(jnp.int32, (slots, slots), 0)
    col = lax.broadcasted_iota(jnp.int32, (slots, slots), 1)
    slot_dots = jnp.sum(jnp.where(row == col, cross, 0.0), axis=0, keepdims=True)
    both_rows = jnp.concatenate([slot_grad, param_ref[...]], axis=0)
    copies = []
    for step in range(tok_ref.shape[0] // chunk):
        part = pl.ds(step * chunk, chunk)
        dispatch = disp_ref[part, :]
        logit_grad = comb_ref[part, :] + dispatch * (disp_cot[part.start : part.start + chunk] - slot_dots)
        weights = jnp.concatenate([dispatch, logit_grad], axis=1).astype(jnp.bfloat16)
        stage[part, :] = dot_nn(weights, both_rows).astype(jnp.bfloat16)
        copy = pltpu.make_async_copy(stage.at[part, :], out_hbm.at[part, :], sems.at[step])
        copy.start()
        copies.append(copy)
    for copy in copies:
        copy.wait()


def stays(value):
    return pltpu.with_memory_space_constraint(value, pltpu.HBM)


def after(value, token):
    return lax.optimization_barrier((value, token))[0]


def seq_bits():
    count = lax.axis_size("seq")
    return [1 << place for place in reversed(range(count.bit_length() - 1))]


def swap(value, bit):
    count = lax.axis_size("seq")
    return lax.ppermute(value, "seq", [(i, i ^ bit) for i in range(count)])


def stat_places(slots, width):
    groups, per_row = slots // GROUP, width // GROUP
    return [
        [(g * GROUP, (v * groups + g) // per_row, (v * groups + g) % per_row * GROUP) for g in range(groups)]
        for v in range(4)
    ]


def stat_rows(slots, width):
    return -(-4 * slots // (16 * width)) * 16


def side_kernel(
    parts, logit_hbm, tok_hbm, param_hbm, slot_hbm, feed_hbm, in_hbm, out_hbm,
    pack_ref, slope_ref, kept_ref, logit_ref, tok_ref, feed_ref, stat_ref, in_ref, sems
):
    slots, width = logit_ref.shape[1], tok_ref.shape[1]
    seq_slots = slot_hbm.shape[0]
    hid = in_hbm.shape[1]
    places = [pl.ds(part * (hid // parts), hid // parts) for part in range(parts)]
    copies = fetch(
        [
            (logit_hbm, logit_ref),
            (tok_hbm, tok_ref),
            (param_hbm, pack_ref.at[pl.ds(slots, seq_slots)]),
            (slot_hbm, pack_ref.at[pl.ds(slots + seq_slots, seq_slots)]),
            (feed_hbm, feed_ref),
        ]
        + [(in_hbm.at[:, at], in_ref.at[:, at]) for at in places]
        + [(out_hbm.at[pl.ds(0, kept_ref.shape[0])], kept_ref)],
        sems,
    )
    copies[0].wait()
    scores = logit_ref[...].astype(jnp.float32)
    highest = jnp.max(scores, axis=0, keepdims=True)
    raised = jnp.exp(scores - highest)
    total = jnp.sum(raised, axis=0, keepdims=True)
    part0 = total.astype(jnp.bfloat16).astype(jnp.float32)
    part1 = (total - part0).astype(jnp.bfloat16).astype(jnp.float32)
    part2 = total - part0 - part1
    stat_ref[...] = jnp.zeros_like(stat_ref)
    for vector, spots in zip((highest, part0, part1, part2), stat_places(slots, width)):
        for slot, row, lane in spots:
            stat_ref[row : row + 1, lane : lane + GROUP] = vector[:, slot : slot + GROUP]
    pack_ref[slots + 2 * seq_slots :] = stat_ref[...].astype(jnp.bfloat16)
    copies[1].wait()
    pack_ref[:slots] = dot_tn(raised.astype(jnp.bfloat16), tok_ref[...]).astype(jnp.bfloat16)
    copies[4].wait()
    feed = [feed_ref[clip].astype(jnp.float32) for clip in range(feed_ref.shape[0])]
    feed = jnp.concatenate(feed, axis=0).astype(jnp.bfloat16)
    root = math.sqrt(2.0 / math.pi)
    for at, copy in zip(places, copies[5:]):
        copy.wait()
        x = dot_nn(feed, in_ref[:, at])
        bend = jnp.tanh(root * (x + 0.044715 * (x * x * x)))
        grown = root * (1.0 + 3.0 * 0.044715 * (x * x))
        slope = 0.5 * (1.0 + bend) + 0.5 * x * (1.0 - bend * bend) * grown
        slope_ref[:, at] = slope.astype(slope_ref.dtype)
    copies[2].wait()
    copies[3].wait()
    copies[-1].wait()


def weight_kernel(seqs, me_ref, logit_hbm, grad_hbm, *refs):
    packs, (disp_ref, comb_ref, sum_ref, param_ref) = list(refs[:seqs]), refs[seqs + 1 : seqs + 5]
    slot_ref, logit_ref, grad_ref, early_ref, sems = refs[seqs + 5 :]
    slots, width = logit_ref.shape[1], grad_ref.shape[1]
    early = [(packs[other], early_ref.at[other // 2]) for other in range(0, seqs, 2)]
    got_logits, *got_early, got_grad = fetch(
        [(logit_hbm, logit_ref)] + early + [(grad_hbm, grad_ref)], sems
    )
    got_logits.wait()
    scores = logit_ref[...].astype(jnp.float32)
    raised = jnp.exp(scores - jnp.max(scores, axis=1, keepdims=True))
    combine = raised / jnp.sum(raised, axis=1, keepdims=True)
    for other in range(0, seqs, 2):
        got_early[other // 2].wait()
        packs[other] = early_ref.at[other // 2]
    seq_slots = slots // seqs
    me = me_ref[0]
    stats = []
    for other, pack in enumerate(packs):
        base = slots + 2 * seq_slots
        rows = pack[base : base + stat_rows(slots, width)].astype(jnp.float32)
        parts = [
            jnp.concatenate([rows[r : r + 1, lane : lane + GROUP] for _, r, lane in places], axis=1)
            for places in stat_places(slots, width)
        ]
        stats.append((parts[0], parts[1] + parts[2] + parts[3]))
        at = pl.ds(pl.multiple_of((me ^ other) * seq_slots, seq_slots), seq_slots)
        param_ref[at, :] = pack[slots : slots + seq_slots]
        slot_ref[at, :] = pack[slots + seq_slots : slots + 2 * seq_slots]
    highest = functools.reduce(jnp.maximum, [top for top, _ in stats])
    total = sum(part * jnp.exp(top - highest) for top, part in stats)
    row = lax.broadcasted_iota(jnp.int32, (slots, slots), 0)
    col = lax.broadcasted_iota(jnp.int32, (slots, slots), 1)
    token_sum = jnp.zeros((slots, width), jnp.float32)
    for pack, (top, _) in zip(packs, stats):
        share = jnp.exp(top - highest) / total
        share = jnp.sum(jnp.where(row == col, share, 0.0), axis=1, keepdims=True)
        token_sum += share * pack[:slots].astype(jnp.float32)
    sum_ref[...] = token_sum.astype(jnp.bfloat16)
    disp_ref[...] = jnp.exp(scores - highest) / total
    got_grad.wait()
    comb_cot = dot_nt(grad_ref[...], slot_ref[...])
    comb_ref[...] = combine * (comb_cot - jnp.sum(combine * comb_cot, axis=1, keepdims=True))


def on_device(
    tokens, out_grad, saved_logits, slot_params, slot_inputs, slot_outputs, expert_in, expert_out
):
    clip_count = lax.axis_size("clip")
    seq_count = lax.axis_size("seq")
    device_count = clip_count * seq_count
    there, back = (exchange_order(device_count, *seed) for seed in SHUFFLES)
    tok_feats, out_cot, logit_raw = tokens[0], out_grad[0], saved_logits[0]
    token_total, width = tok_feats.shape
    slot_total = logit_raw.shape[1]
    clip_total, local_slots = slot_inputs.shape[:2]
    hid = expert_in.shape[2]
    feed_rows = clip_total * local_slots
    f32, b16 = jnp.float32, jnp.bfloat16

    still_logits, still_grad = stays(logit_raw), stays(out_cot)
    still_in, still_out = stays(expert_in[0]), stays(expert_out[0])
    blocks = pl.pallas_call(
        functools.partial(cot_kernel, there),
        out_shape=jax.ShapeDtypeStruct((device_count, local_slots, width), b16),
        in_specs=[STAYS, STAYS],
        out_specs=WHOLE,
        scratch_shapes=[
            pltpu.VMEM((token_total, slot_total), b16),
            pltpu.VMEM((token_total, width), b16),
            pltpu.SemaphoreType.DMA((2,)),
        ],
        compiler_params=pltpu.CompilerParams(vmem_limit_bytes=16 * MIB),
        cost_estimate=FREE,
    )(still_logits, still_grad)
    received = exchange(blocks, there)

    parts = math.gcd(hid // GROUP, 3)
    seq_slots = slot_params.shape[1]
    pack_rows = slot_total + 2 * seq_slots + stat_rows(slot_total, width)
    pieces = math.gcd(hid // GROUP, 6)
    chunk, wide = hid // pieces, hid // math.gcd(pieces, 3)
    kept_rows = max(pieces // 2, 1) * chunk
    own, slope, kept = pl.pallas_call(
        functools.partial(side_kernel, parts),
        out_shape=(
            jax.ShapeDtypeStruct((pack_rows, width), b16),
            jax.ShapeDtypeStruct((feed_rows, hid), b16),
            pltpu.VMEM((kept_rows, width), b16),
        ),
        in_specs=[STAYS] * 7,
        out_specs=(WHOLE,) * 3,
        scratch_shapes=[
            pltpu.VMEM((token_total, slot_total), b16),
            pltpu.VMEM((token_total, width), b16),
            pltpu.VMEM(slot_inputs.shape, b16),
            pltpu.VMEM((stat_rows(slot_total, width), width), f32),
            pltpu.VMEM((width, hid), b16),
            pltpu.SemaphoreType.DMA((6 + parts,)),
        ],
        compiler_params=pltpu.CompilerParams(vmem_limit_bytes=24 * MIB),
        cost_estimate=FREE,
    )(
        still_logits,
        stays(tok_feats),
        stays(slot_params.T),
        stays(slot_outputs[0]),
        stays(slot_inputs),
        still_in,
        still_out,
    )

    send = pl.pallas_call(
        functools.partial(expert_kernel, there, back, clip_count, seq_count, chunk, wide),
        out_shape=jax.ShapeDtypeStruct((device_count, local_slots, width), b16),
        in_specs=[WHOLE, WHOLE, WHOLE, STAYS, STAYS],
        out_specs=WHOLE,
        scratch_shapes=[
            pltpu.VMEM((width, hid), b16),
            pltpu.VMEM((max(hid - kept_rows, chunk), width), b16),
            pltpu.VMEM((feed_rows, hid), b16),
            pltpu.SemaphoreType.DMA(((hid - kept_rows) // chunk + hid // wide,)),
        ],
        compiler_params=pltpu.CompilerParams(vmem_limit_bytes=20 * MIB),
        cost_estimate=pl.CostEstimate(
            flops=4 * feed_rows * width * hid,
            bytes_accessed=4 * width * hid,
            transcendentals=0,
        ),
    )(
        received,
        pltpu.with_memory_space_constraint(kept, pltpu.VMEM),
        slope,
        still_in,
        still_out,
    )
    returned = exchange(send, back)

    held = {0: own}
    for bit in seq_bits():
        for other in list(held):
            held[other ^ bit] = swap(held[other] if other == 0 else after(held[other], send), bit)
    dispatch, comb_logit, token_sum, param_all = pl.pallas_call(
        functools.partial(weight_kernel, seq_count),
        out_shape=(
            jax.ShapeDtypeStruct((token_total, slot_total), f32),
            jax.ShapeDtypeStruct((token_total, slot_total), f32),
            jax.ShapeDtypeStruct((slot_total, width), b16),
            jax.ShapeDtypeStruct((slot_total, width), b16),
        ),
        in_specs=[pl.BlockSpec(memory_space=pltpu.SMEM), STAYS, STAYS]
        + [STAYS if other % 2 == 0 else WHOLE for other in range(seq_count)]
        + [PLACED],
        out_specs=(WHOLE,) * 4,
        scratch_shapes=[
            pltpu.VMEM((slot_total, width), b16),
            pltpu.VMEM((token_total, slot_total), b16),
            pltpu.VMEM((token_total, width), b16),
            pltpu.VMEM(((seq_count + 1) // 2, pack_rows, width), b16),
            pltpu.SemaphoreType.DMA((2 + (seq_count + 1) // 2,)),
        ],
        compiler_params=pltpu.CompilerParams(vmem_limit_bytes=48 * MIB),
        cost_estimate=FREE,
    )(
        lax.axis_index("seq")[None],
        still_logits,
        still_grad,
        *[stays(held[at]) if at % 2 == 0 else held[at] for at in range(seq_count)],
        send,
    )

    step = math.gcd(token_total, 128)
    token_grad = pl.pallas_call(
        functools.partial(token_kernel, back, step),
        out_shape=jax.ShapeDtypeStruct((token_total, width), b16),
        in_specs=[WHOLE] * 6,
        out_specs=PLACED,
        scratch_shapes=[
            pltpu.VMEM((token_total, width), b16),
            pltpu.SemaphoreType.DMA((token_total // step,)),
        ],
        compiler_params=pltpu.CompilerParams(vmem_limit_bytes=16 * MIB),
        cost_estimate=pl.CostEstimate(
            flops=6 * token_total * width * slot_total,
            bytes_accessed=4 * token_total * width,
            transcendentals=0,
        ),
    )(
        tok_feats,
        returned,
        token_sum,
        dispatch,
        comb_logit,
        param_all,
    )
    return token_grad[None]


def solution(mesh):
    placed = (
        P("clip", "seq", None),
        P("clip", "seq", None),
        P("clip", "seq", None),
        P(None, "seq"),
        P(None, BOTH, None),
        P("clip", "seq", None),
        P(BOTH, None, None),
        P(BOTH, None, None),
    )
    return jax.shard_map(
        on_device, mesh=mesh, in_specs=placed, out_specs=P("clip", "seq", None), check_vma=False
    )
```
